128 devices in a mesh: gx: 8 (over x, core), gy: 16 (over y, z).
Axes of the slice: x: 4, y: 4, z: 4, core: 2. Of those that a mesh axis runs over, the one named last changes fastest.
Arguments:
- displacement: float32 [6, 1048576], P(None, ('gx', 'gy')), may hold values from -4 to 4
- velocity: float32 [6, 1048576], P(None, ('gx', 'gy')), may hold values from -6 to 6
- ref_pos: float32 [3, 1048576], P(None, ('gx', 'gy')), may hold values from -6 to 6
- normals: float32 [3, 1048576], P(None, ('gx', 'gy')), may hold values from -4 to 4
- inv_mass: float32 [6, 1048576], P(None, ('gx', 'gy')), may hold values from 0.5 to 2
- connectivity: int32 [4, 1048576], P(None, ('gx', 'gy')), may hold values from 0 to 8191, as said below
- stiffness: bfloat16 [24, 24, 1048576], P(None, None, ('gx', 'gy'))
- yield_force: float32 [1048576], P(('gx', 'gy')), may hold values from 2 to 20
- shared_nodes: int32 [4, 16384], P(None, ('gx', 'gy')), may hold values from 0 to 8191, as said below
- block_slot: int32 [8192], P(('gx', 'gy')), may hold values from 0 to 255, as said below
- edge_slots: int32 [1024], P(('gx', 'gy')), may hold values from 0 to 255, as said below
- tile_pairs: int32 [2, 32768], P(None, ('gx', 'gy')), may hold values from 0 to 287, as said below
- tile_count: int32 [128], P(('gx', 'gy')), may hold values from 0 to 256, as said below
- win_start: int32 [32768, 128], P(('gx', 'gy')), may hold values from 0 to 127
- win_len: int32 [32768, 128], P(('gx', 'gy')), may hold values from 1 to 128
Outputs:
- displacement_out: float32 [6, 1048576], P(None, ('gx', 'gy'))
- velocity_out: float32 [6, 1048576], P(None, ('gx', 'gy'))
The draws below stay inside these ranges and needn't reach their ends.
Inputs may be any that keep to these rules, and one draw needn't show every extreme that they name: `connectivity`: element e of a partition (e counted within the partition) has its corners among the partition's nodes 128 * (e // 128) to 128 * (e // 128) + 127. `shared_nodes`: the four rows of a partition list distinct local nodes, 128 a row, 512 distinct in all. `block_slot`: entries of one partition are distinct; box = entry // 2 is the receiving box. Every partition fills all 2 places of some boxes, and some boxes receive 2 blocks from every partition. `edge_slots`: places of a box's received blocks. `tile_pairs`: row 0 is a received place; row 1 is a received place or 256 + k for entry k of the neighbours' edge blocks. A box uses its first tile_count tiles; some box uses all 256 in every draw.
All inputs are finite; a program needn't handle non-finite values.
Results may differ from the reference program's by a relative error of at most 0.0003.
Values sent between devices are 32-bit elements; how exact they have to be, the bound alone decides.
A program may use at most 128 MiB of HBM per device.

```python
import math
import jax
import jax.numpy as jnp
from jax import lax

BLK = 128
SBLK_DEV = 64
CAP = 2
EDGE = 8
SHARE = 128
STEPS = 2
NODE_DEV = 8192
NODES = 1048576
ELEMS = 1048576
TILES_DEV = 256
TILES = 32768
N_GX = 8
N_GY = 16


def routing_plan(key):
    devices = N_GX * N_GY
    slot_total = devices * CAP
    hot_number = max(1, SBLK_DEV // (4 * CAP))
    base_key = jax.random.fold_in(key, 7001)
    boxes_order = jax.random.permutation(jax.random.fold_in(base_key, 1), devices)
    hot_flag = jnp.zeros((devices,), jnp.int32).at[boxes_order[:hot_number]].set(1)
    slot_hot = jnp.repeat(hot_flag, CAP)
    source_keys = jax.random.split(jax.random.fold_in(base_key, 2), devices)

    def pick_slots(one_key):
        key_score, key_order = jax.random.split(one_key)
        slot_score = jax.random.randint(key_score, (slot_total,), 0, 1 << 20) + slot_hot * (1 << 21)
        slot_score = slot_score * slot_total + jnp.arange(slot_total, dtype=jnp.int32)
        chosen = jnp.argsort(-slot_score)[:SBLK_DEV]
        return jax.random.permutation(key_order, chosen).astype(jnp.int32)
    return jax.vmap(pick_slots)(source_keys)


def contact_plan(key):
    devices = N_GX * N_GY
    slot_total = devices * CAP
    routed = routing_plan(key)
    box_of = routed // CAP
    within = routed % CAP
    source = jnp.arange(devices, dtype=jnp.int32)[:, None]
    occupied = jnp.zeros((devices, slot_total), jnp.int32).at[box_of, source * CAP + within].set(1)
    live_count = jnp.sum(occupied, axis=1)
    plan_key = jax.random.fold_in(key, 7002)
    noise = jax.random.randint(jax.random.fold_in(plan_key, 1), (devices, slot_total), 0, 1 << 10)
    order_score = (occupied * (1 << 20) + noise) * slot_total + jnp.arange(slot_total, dtype=jnp.int32)[None, :]
    live_order = jnp.argsort(-order_score, axis=1).astype(jnp.int32)
    safe_count = jnp.maximum(live_count, 1)
    tile_index = jnp.arange(TILES_DEV, dtype=jnp.int32)
    slave_pos = tile_index[None, :] // 2 % safe_count[:, None]
    slaves = jnp.take_along_axis(live_order, slave_pos, axis=1)
    own_pick = jax.random.randint(jax.random.fold_in(plan_key, 2), (devices, TILES_DEV), 0, 1 << 20) % safe_count[:, None]
    own_master = jnp.take_along_axis(live_order, own_pick, axis=1)
    edge_master = slot_total + jax.random.randint(jax.random.fold_in(plan_key, 3), (devices, TILES_DEV), 0, 4 * EDGE)
    masters = jnp.where(tile_index[None, :] % 2 == 0, own_master, edge_master)
    counts = jnp.minimum(2 * live_count, TILES_DEV)
    edge_pos = jnp.arange(EDGE, dtype=jnp.int32)[None, :] % safe_count[:, None]
    edges = jnp.take_along_axis(live_order, edge_pos, axis=1)
    return (slaves.astype(jnp.int32), masters.astype(jnp.int32), counts.astype(jnp.int32), edges.astype(jnp.int32))


def draw_connectivity(key, part):
    local = jax.random.randint(jax.random.fold_in(key, 7005), (4, ELEMS), 0, BLK)
    local = local.at[0, 0].set(0)
    local = local.at[0, ELEMS - 1].set(BLK - 1)
    element = jnp.arange(ELEMS, dtype=jnp.int32) % NODE_DEV
    return (element // BLK * BLK)[None, :] + local.astype(jnp.int32)


def draw_block_slot(key, part):
    return routing_plan(key).reshape(-1)


def draw_tile_pairs(key, part):
    slaves, masters, counts, edges = contact_plan(key)
    stacked = jnp.stack([slaves, masters], axis=1)
    return jnp.transpose(stacked, (1, 0, 2)).reshape(2, -1)


def draw_tile_count(key, part):
    slaves, masters, counts, edges = contact_plan(key)
    return counts


def draw_edge_slots(key, part):
    slaves, masters, counts, edges = contact_plan(key)
    return edges.reshape(-1)


def draw_shared_nodes(key, part):
    devices = N_GX * N_GY
    node_keys = jax.random.split(jax.random.fold_in(key, 7003), devices)

    def pick_nodes(one_key):
        return jax.random.permutation(one_key, NODE_DEV)[:4 * SHARE].reshape(4, SHARE)
    lists = jax.vmap(pick_nodes)(node_keys)
    return jnp.transpose(lists, (1, 0, 2)).reshape(4, -1).astype(jnp.int32)


def draw_stiffness(key, part):
    noise = jax.random.normal(jax.random.fold_in(key, 7004), (24, 24, ELEMS), jnp.float32) * 0.25
    diagonal = 1.5 * jnp.eye(24, dtype=jnp.float32)[:, :, None]
    return (noise + diagonal).astype(jnp.bfloat16)


def plant(array, own_key, low, largest):
    place = [jax.random.randint(jax.random.fold_in(own_key, axis), (), 0, length) for axis, length in enumerate(array.shape)]
    widest = array.shape.index(max(array.shape))
    beside = place[:widest] + [(place[widest] + 1) % array.shape[widest]] + place[widest + 1:]
    return array.at[tuple(place)].set(low).at[tuple(beside)].set(largest)


def shard_levels(own_key, extent, shards, smallest, largest):
    def one(axis_at, blocks):
        draws = jax.random.uniform(jax.random.fold_in(jax.random.fold_in(own_key, 6), axis_at), (blocks,), jnp.float32, smallest / len(shards), largest / len(shards))
        return jnp.repeat(jnp.exp(draws), extent[axis_at] // blocks).reshape((-1,) + (1,) * (len(extent) - axis_at - 1))

    level = one(*shards[0])
    for cut in shards[1:]:
        level = level * one(*cut)
    return level


def gaussian(key, dims, scale, most, cuts=(), held_as=jnp.bfloat16):
    gain = shard_levels(key, dims, cuts, -0.22, 0.18) if cuts else 1.0
    array = jax.random.normal(key, dims, jnp.float32) * scale * gain
    return jnp.minimum(jnp.maximum(array, -most), most).astype(held_as)


def setup_inputs(seed: int = 0) -> dict:
    key_list = jax.random.split(jax.random.key(seed), 16)
    displacement = gaussian(key_list[0], (6, NODES), 0.5, 4.0, ((1, 128),), jnp.float32)
    velocity = gaussian(key_list[1], (6, NODES), 1.0, 6.0, ((1, 128),), jnp.float32)
    ref_pos = gaussian(key_list[2], (3, NODES), 1.0, 6.0, ((1, 128),), jnp.float32)
    normals = gaussian(key_list[3], (3, NODES), 0.6, 4.0, ((1, 128),), jnp.float32)
    inv_mass = jnp.clip(jnp.exp(math.log(2.0) - 1.3862944 * jax.random.uniform(key_list[4], (6, NODES), jnp.float32) ** shard_levels(key_list[4], (6, NODES), ((1, 128),), -0.2, 0.2)), 0.5, 2.0)
    connectivity = draw_connectivity(jax.random.fold_in(key_list[15], 71), 0)
    stiffness = draw_stiffness(jax.random.fold_in(key_list[15], 71), 0)
    yield_force = jnp.clip(jnp.exp(math.log(20.0) - 2.3025851 * jax.random.uniform(key_list[7], (ELEMS,), jnp.float32) ** shard_levels(key_list[7], (ELEMS,), ((0, 128),), -0.2, 0.2)), 2.0, 20.0)
    shared_nodes = draw_shared_nodes(jax.random.fold_in(key_list[15], 71), 0)
    block_slot = draw_block_slot(jax.random.fold_in(key_list[15], 71), 0)
    edge_slots = draw_edge_slots(jax.random.fold_in(key_list[15], 71), 0)
    tile_pairs = draw_tile_pairs(jax.random.fold_in(key_list[15], 71), 0)
    tile_count = draw_tile_count(jax.random.fold_in(key_list[15], 71), 0)
    win_start = plant(jax.random.randint(key_list[13], (TILES, BLK), 0, BLK), jax.random.fold_in(key_list[13], 1), 0, BLK - 1).astype(jnp.int32)
    win_len = plant(jax.random.randint(key_list[14], (TILES, BLK), 1, BLK + 1), jax.random.fold_in(key_list[14], 1), 1, BLK).astype(jnp.int32)
    return dict(displacement=displacement, velocity=velocity, ref_pos=ref_pos, normals=normals, inv_mass=inv_mass, connectivity=connectivity, stiffness=stiffness, yield_force=yield_force, shared_nodes=shared_nodes, block_slot=block_slot, edge_slots=edge_slots, tile_pairs=tile_pairs, tile_count=tile_count, win_start=win_start, win_len=win_len)


TIME_STEP = 0.5
PENALTY = 32.0
THICKNESS = 0.2

def element_forces(displacement, connectivity, stiffness, yield_force):
    node_count = displacement.shape[1]
    gathered = displacement[:, connectivity]
    elem_dofs = gathered.reshape(24, -1)
    trial = lax.optimization_barrier(jnp.sum(stiffness.astype(jnp.float32) * elem_dofs[None, :, :], axis=1))
    squared = lax.optimization_barrier(jnp.sum(trial * trial, axis=0))
    factor = 1.0 / jnp.sqrt(1.0 + squared / (yield_force * yield_force))
    element_force = (trial * factor[None, :]).reshape(6, 4, -1)
    internal = jnp.zeros((6, node_count), jnp.float32)
    for corner in range(4):
        internal = internal.at[:, connectivity[corner]].add(element_force[:, corner])
    return internal

def tile_forces(own_blocks, extended, slaves, masters, starts, lengths, active):
    width = own_blocks.shape[2]
    slave_pos = own_blocks[0:3][:, slaves]
    master_pos = extended[0:3][:, masters]
    master_nrm = extended[3:6][:, masters]
    offset = lax.optimization_barrier(jnp.sum(master_pos * master_nrm, axis=0))
    gap_matrix = jnp.einsum('cti,ctj->tij', slave_pos, master_nrm, precision=lax.Precision.HIGHEST) - offset[:, None, :]
    column = jnp.arange(width, dtype=jnp.int32)
    inside = (column[None, None, :] - starts[:, :, None]) % width < lengths[:, :, None]
    inside = jnp.logical_and(inside, active[:, None, None])
    pressure = jnp.where(inside, jnp.maximum(THICKNESS - gap_matrix, 0.0), 0.0)
    return PENALTY / width * jnp.einsum('tij,ctj->cti', pressure, master_nrm, precision=lax.Precision.HIGHEST)

def fetch(blocks, owner, box_index, rows):
    source = rows // CAP
    slot_place = rows % CAP
    block_index = owner[source, box_index * CAP + slot_place]
    present = block_index >= 0
    global_index = source * SBLK_DEV + jnp.maximum(block_index, 0)
    block_data = jnp.where(present[None, :, None], blocks[:, global_index], 0.0)
    return (block_data, global_index, present)

def side_values(force_dev, lists_dev):
    return force_dev[:, lists_dev]

def place_sides(force_dev, lists_dev, incoming_dev):
    for side in range(4):
        force_dev = force_dev.at[:, lists_dev[side]].add(incoming_dev[:, side])
    return force_dev

def reference(displacement, velocity, ref_pos, normals, inv_mass, connectivity, stiffness, yield_force, shared_nodes, block_slot, edge_slots, tile_pairs, tile_count, win_start, win_len):
    devices = N_GX * N_GY
    slot_total = devices * CAP
    node_dev = SBLK_DEV * BLK
    device_ids = jnp.arange(devices, dtype=jnp.int32)
    owner = jnp.full((devices, slot_total), -1, jnp.int32)
    owner = owner.at[device_ids[:, None], block_slot.reshape(devices, SBLK_DEV)].set(jnp.arange(SBLK_DEV, dtype=jnp.int32)[None, :])
    all_rows = jnp.arange(slot_total, dtype=jnp.int32)
    for time_step in range(STEPS):

        def per_device(index):
            start = index * node_dev
            disp_dev = lax.dynamic_slice_in_dim(displacement, start, node_dev, 1)
            conn_dev = lax.dynamic_slice_in_dim(connectivity, start, node_dev, 1)
            stiff_dev = lax.dynamic_slice_in_dim(stiffness, start, node_dev, 2)
            yield_dev = lax.dynamic_slice_in_dim(yield_force, start, node_dev, 0)
            return element_forces(disp_dev, conn_dev, stiff_dev, yield_dev)
        internal = lax.map(per_device, device_ids)
        internal = jnp.transpose(internal, (1, 0, 2)).reshape(6, -1)
        positions = ref_pos + displacement[0:3]
        blocks = jnp.concatenate([positions, normals], axis=0).reshape(6, devices * SBLK_DEV, BLK)

        def per_box(running, box_index):
            box_row = box_index // N_GY
            box_col = box_index % N_GY
            own_blocks, own_index, own_present = fetch(blocks, owner, box_index, all_rows)
            pieces = [own_blocks]
            for row_step, col_step in ((-1, 0), (1, 0), (0, -1), (0, 1)):
                near_row = box_row + row_step
                near_col = box_col + col_step
                exists = (near_row >= 0) & (near_row < N_GX) & (near_col >= 0) & (near_col < N_GY)
                near_box = jnp.clip(near_row, 0, N_GX - 1) * N_GY + jnp.clip(near_col, 0, N_GY - 1)
                edge_list = lax.dynamic_slice_in_dim(edge_slots, near_box * EDGE, EDGE, 0)
                edge_data, unused_index, unused_present = fetch(blocks, owner, near_box, edge_list)
                pieces.append(jnp.where(exists, edge_data, 0.0))
            extended = jnp.concatenate(pieces, axis=1)
            tile_rows = lax.dynamic_slice_in_dim(tile_pairs, box_index * TILES_DEV, TILES_DEV, 1)
            starts = lax.dynamic_slice_in_dim(win_start, box_index * TILES_DEV, TILES_DEV, 0)
            lengths = lax.dynamic_slice_in_dim(win_len, box_index * TILES_DEV, TILES_DEV, 0)
            active = jnp.arange(TILES_DEV, dtype=jnp.int32) < tile_count[box_index]
            forces = tile_forces(own_blocks, extended, tile_rows[0], tile_rows[1], starts, lengths, active)
            box_force = jnp.zeros((3, slot_total, BLK), jnp.float32).at[:, tile_rows[0]].add(forces)
            box_force = jnp.where(own_present[None, :, None], box_force, 0.0)
            running = running.at[:, own_index].add(box_force)
            return (running, None)
        contact, unused = lax.scan(per_box, jnp.zeros((3, devices * SBLK_DEV, BLK), jnp.float32), device_ids)
        contact_nodes = contact.reshape(3, -1)
        nodal_force = jnp.concatenate([contact_nodes, jnp.zeros_like(contact_nodes)], axis=0) - internal
        force_grid = nodal_force.reshape(6, devices, node_dev)
        lists = shared_nodes.reshape(4, devices, SHARE)
        sides = jax.vmap(side_values, in_axes=(1, 1), out_axes=1)(force_grid, lists)
        grid = sides.reshape(6, N_GX, N_GY, 4, SHARE)
        from_west = jnp.pad(grid[:, :-1, :, 1], ((0, 0), (1, 0), (0, 0), (0, 0)))
        from_east = jnp.pad(grid[:, 1:, :, 0], ((0, 0), (0, 1), (0, 0), (0, 0)))
        from_south = jnp.pad(grid[:, :, :-1, 3], ((0, 0), (0, 0), (1, 0), (0, 0)))
        from_north = jnp.pad(grid[:, :, 1:, 2], ((0, 0), (0, 0), (0, 1), (0, 0)))
        incoming = jnp.stack([from_west, from_east, from_south, from_north], axis=3).reshape(6, devices, 4, SHARE)
        assembled = jax.vmap(place_sides, in_axes=(1, 1, 1), out_axes=1)(force_grid, lists, incoming).reshape(6, -1)
        velocity = velocity + TIME_STEP * inv_mass * assembled
        displacement = displacement + TIME_STEP * velocity
    return (displacement, velocity)
```

```python
import functools

import jax
import jax.numpy as jnp
from jax import lax
from jax.experimental import pallas as pl
from jax.experimental.pallas import tpu as pltpu
from jax.sharding import PartitionSpec as P

BLK = 128
CAP = 2
STEPS = 2
TIME_STEP = 0.5
PENALTY = 32.0
THICKNESS = 0.2
F32 = jnp.float32
BF16 = jnp.bfloat16
VMEM = pl.BlockSpec(memory_space=pltpu.VMEM)
SMEM = pl.BlockSpec(memory_space=pltpu.SMEM)
LIMIT = 48 * 1024 * 1024


def rows_iota():
    return lax.broadcasted_iota(jnp.int32, (8, BLK), 0)


def merge_rows(even, odd, bit):
    low = (rows_iota() & bit) == 0
    return jnp.where(low, even, odd) + pltpu.roll(jnp.where(low, odd, even), bit, 0)


def sum_six(parts):
    first = [merge_rows(parts[2 * m], parts[2 * m + 1], 1) for m in range(3)]
    upper = first[2] + pltpu.roll(first[2], 2, 0)
    return merge_rows(merge_rows(first[0], first[1], 2), upper, 4)


def split(value):
    high = value.astype(BF16).astype(F32)
    return high, value - high


def lanes(value, index):
    return jnp.take_along_axis(value, index, axis=1)


def element_block(disp, corner, load_stiff, limit):
    index = jnp.concatenate([corner, corner], axis=0)
    dofs = []
    for pair in range(3):
        source = jnp.concatenate(
            [
                jnp.broadcast_to(disp[2 * pair : 2 * pair + 1], (4, BLK)),
                jnp.broadcast_to(disp[2 * pair + 1 : 2 * pair + 2], (4, BLK)),
            ],
            axis=0,
        )
        dofs.append(lanes(source, index))
    trial = []
    for a in range(4):
        parts = []
        for c in range(6):
            row = load_stiff(4 * c + a).astype(F32)
            parts.append(row[0:8] * dofs[0] + row[8:16] * dofs[1] + row[16:24] * dofs[2])
        trial.append(sum_six(parts))
    squares = trial[0] * trial[0] + trial[1] * trial[1] + trial[2] * trial[2] + trial[3] * trial[3]
    squared = jnp.sum(jnp.where(rows_iota() < 6, squares, 0.0), axis=0, keepdims=True)
    factor = 1.0 / jnp.sqrt(1.0 + squared / (limit * limit))
    node = lax.broadcasted_iota(jnp.int32, (BLK, BLK), 0)
    left = []
    right = []
    for a in range(4):
        high, low = split(trial[a] * factor)
        left.append(jnp.concatenate([high, low], axis=0).astype(BF16))
        right.append(jnp.where(node == corner[a : a + 1], 1.0, 0.0).astype(BF16))
    both = lax.dot_general(
        jnp.concatenate(left, axis=1),
        jnp.concatenate(right, axis=1),
        (((1,), (1,)), ((), ())),
        preferred_element_type=F32,
    )
    return both[0:8] + both[8:16]


def element_kernel(disp_ref, corner_ref, stiff_ref, limit_ref, out_ref):
    blocks = out_ref.shape[0]

    def one(k, carry):
        where = pl.ds(pl.multiple_of(k * BLK, BLK), BLK)
        out_ref[k] = element_block(
            disp_ref[:, where],
            corner_ref[:, where] & (BLK - 1),
            lambda i: stiff_ref[i, :, where],
            limit_ref[pl.ds(k, 1)],
        )
        return carry

    lax.fori_loop(0, blocks, one, 0, unroll=2)


def element_forces(disp, connectivity, stiffness, limit):
    count = limit.shape[0]
    step = 8
    width = step * BLK
    return pl.pallas_call(
        element_kernel,
        grid=(count // step,),
        in_specs=[
            pl.BlockSpec((6, width), lambda g: (0, g)),
            pl.BlockSpec((4, width), lambda g: (0, g)),
            pl.BlockSpec((24, 24, width), lambda g: (0, 0, g)),
            pl.BlockSpec((step, BLK), lambda g: (g, 0)),
        ],
        out_specs=pl.BlockSpec((step, 8, BLK), lambda g: (g, 0, 0)),
        out_shape=jax.ShapeDtypeStruct((count, 8, BLK), F32),
        compiler_params=pltpu.CompilerParams(vmem_limit_bytes=LIMIT),
        cost_estimate=pl.CostEstimate(
            flops=2 * 576 * count * BLK, bytes_accessed=1152 * count * BLK, transcendentals=0
        ),
        name="elements",
    )(disp, connectivity, stiffness, limit)


def node_table(pos):
    full = jnp.concatenate([pos, pos, jnp.ones((2, BLK), F32)], axis=0)
    high, low = split(full)
    return jnp.concatenate([high, low], axis=0).astype(BF16)


def facet_table(pos, nrm):
    offset = jnp.sum(pos * nrm, axis=0, keepdims=True) + THICKNESS
    nrm_high, nrm_low = split(-nrm)
    off_high, off_low = split(offset)
    half = jnp.concatenate([nrm_high, nrm_low, off_high, off_low], axis=0)
    return jnp.concatenate([half, half], axis=0).astype(BF16)


def contact_kernel(
    pairs_ref, count_ref, got_ref, edge_ref, slave_ref, start_ref, len_ref, out_ref, node_tab, facet_tab, tile_out
):
    places = got_ref.shape[0]
    tiles = start_ref.shape[0]

    def tables(r, carry):
        block = got_ref[r]
        node_tab[r] = node_table(block[0:3])
        facet_tab[r] = facet_table(block[0:3], block[3:6])
        return carry

    lax.fori_loop(0, places, tables, 0, unroll=4)

    def edge_tables(r, carry):
        block = edge_ref[r]
        facet_tab[places + r] = facet_table(block[0:3], block[3:6])
        return carry

    lax.fori_loop(0, edge_ref.shape[0], edge_tables, 0, unroll=4)

    facet = lax.broadcasted_iota(jnp.int32, (BLK, 2 * BLK), 0) << 25
    zero = jnp.zeros((16, BLK), BF16)
    top = jnp.int32(-(2**31))

    def pair(g, carry):
        t = 2 * g
        left = [facet_tab[pairs_ref[1, t + h]] for h in range(2)]
        right = [node_tab[pairs_ref[0, t + h]] for h in range(2)]
        depth = lax.dot_general(
            jnp.concatenate(left, axis=0),
            jnp.concatenate(
                [
                    jnp.concatenate([right[0], zero], axis=1),
                    jnp.concatenate([zero, right[1]], axis=1),
                ],
                axis=0,
            ),
            (((0,), (0,)), ((), ())),
            preferred_element_type=F32,
        )
        start = jnp.concatenate([start_ref[pl.ds(t + h, 1)] for h in range(2)], axis=1)
        length = jnp.concatenate([len_ref[pl.ds(t + h, 1)] for h in range(2)], axis=1)
        shifted = (start << 25) + top
        last = ((length - 1) << 25) + top
        inside = facet - shifted <= last
        pressure = jnp.where(inside, jnp.maximum(depth, 0.0), 0.0)
        high = pressure.astype(BF16)
        low = (pressure - high.astype(F32)).astype(BF16)
        force = lax.dot_general(
            jnp.concatenate(
                [jnp.concatenate([left[h], left[h]], axis=1) for h in range(2)], axis=0
            ),
            jnp.concatenate([high, low], axis=0),
            (((1,), (0,)), ((), ())),
            preferred_element_type=F32,
        )
        tile_out[pl.ds(pl.multiple_of(8 * t, 16), 8)] = force[0:8, 0:BLK]
        tile_out[pl.ds(pl.multiple_of(8 * t + 8, 8), 8)] = force[16:24, BLK : 2 * BLK]
        return carry

    lax.fori_loop(0, tiles // 2, pair, 0, unroll=2)

    place = lax.broadcasted_iota(jnp.int32, (places, tiles), 0)
    active = lax.broadcasted_iota(jnp.int32, (places, tiles), 1) < count_ref[0]
    pick = jnp.where((place == slave_ref[...]) & active, -PENALTY / BLK, 0.0).astype(BF16)
    for c in range(3):
        total = tile_out[pl.ds(c, tiles, 8)] + tile_out[pl.ds(c + 3, tiles, 8)]
        high, low = split(total)
        both = jnp.dot(
            pick,
            jnp.concatenate([high.astype(BF16), low.astype(BF16)], axis=1),
            preferred_element_type=F32,
        )
        out_ref[c] = both[:, 0:BLK] + both[:, BLK : 2 * BLK]


def contact_forces(pairs, count, got, edges, start, length):
    places, tiles = got.shape[0], start.shape[0]
    extended = places + edges.shape[0]
    return pl.pallas_call(
        contact_kernel,
        in_specs=[SMEM, SMEM] + [VMEM] * 5,
        out_specs=VMEM,
        out_shape=jax.ShapeDtypeStruct((3, places, BLK), F32),
        scratch_shapes=[
            pltpu.VMEM((places, 16, BLK), BF16),
            pltpu.VMEM((extended, 16, BLK), BF16),
            pltpu.VMEM((8 * tiles, BLK), F32),
        ],
        compiler_params=pltpu.CompilerParams(vmem_limit_bytes=LIMIT),
        cost_estimate=pl.CostEstimate(
            flops=2 * tiles * BLK * BLK * 32, bytes_accessed=4 << 20, transcendentals=0
        ),
        name="contact",
    )(pairs, count, got, edges, pairs[0:1], start, length)


def pack_blocks(disp_ref, ref_ref, nrm_ref, back_ref, out_ref, surface):
    blocks = surface.shape[0] - 1
    surface[blocks] = jnp.zeros((8, BLK), F32)
    for k in range(blocks):
        where = slice(k * BLK, (k + 1) * BLK)
        surface[k, 0:3] = ref_ref[:, where] + disp_ref[0:3, where]
        if nrm_ref is not None:
            surface[k, 3:6] = nrm_ref[:, where]

    rows = out_ref.shape[1]

    def place(r, carry):
        out_ref[r] = surface[back_ref[r]][0:rows]
        return carry

    lax.fori_loop(0, out_ref.shape[0], place, 0, unroll=8)


def first_kernel(back_ref, shared_ref, disp_ref, ref_ref, nrm_ref, out_ref, inverse_ref, surface):
    pack_blocks(disp_ref, ref_ref, nrm_ref, back_ref, out_ref, surface)
    blocks = inverse_ref.shape[1]
    block = lax.broadcasted_iota(jnp.int32, (blocks, BLK), 0)
    entry = (lax.broadcasted_iota(jnp.int32, (blocks, BLK), 1) + 1).astype(F32)
    lane = lax.broadcasted_iota(jnp.int32, (BLK, BLK), 0)
    for side in range(4):
        node = shared_ref[side : side + 1]
        found = lax.dot_general(
            jnp.where(block == (node >> 7), entry, 0.0).astype(BF16),
            jnp.where(lane == (node & (BLK - 1)), 1.0, 0.0).astype(BF16),
            (((1,), (1,)), ((), ())),
            preferred_element_type=F32,
        )
        inverse_ref[side] = found.astype(jnp.int32) - 1


def first_pack(back, shared, disp, ref_pos, normals):
    blocks = disp.shape[1] // BLK
    return pl.pallas_call(
        first_kernel,
        in_specs=[SMEM] + [VMEM] * 4,
        out_specs=[VMEM, VMEM],
        out_shape=[
            jax.ShapeDtypeStruct((back.shape[0], 6, BLK), F32),
            jax.ShapeDtypeStruct((4, blocks, BLK), jnp.int32),
        ],
        scratch_shapes=[pltpu.VMEM((blocks + 1, 8, BLK), F32)],
        compiler_params=pltpu.CompilerParams(vmem_limit_bytes=LIMIT),
        name="first_pack",
    )(back, shared, disp, ref_pos, normals)


def force_kernel(slot_ref, shared_ref, internal_ref, back_ref, force_ref, side_ref):
    blocks = internal_ref.shape[0]
    node = [jnp.broadcast_to(shared_ref[s : s + 1], (8, BLK)) for s in range(4)]
    block = [n >> 7 for n in node]
    lane = [n & (BLK - 1) for n in node]
    found = [jnp.zeros((8, BLK), F32) for s in range(4)]
    none = jnp.zeros((5, BLK), F32)
    for k in range(blocks):
        contact = jnp.concatenate([back_ref[slot_ref[k]], none], axis=0)
        force = contact - internal_ref[k]
        force_ref[k] = force
        for s in range(4):
            found[s] = jnp.where(block[s] == k, lanes(force, lane[s]), found[s])
    for s in range(4):
        side_ref[s] = found[s][0:6]


def nodal_forces(slot, shared, internal, returned):
    blocks = internal.shape[0]
    return pl.pallas_call(
        force_kernel,
        in_specs=[SMEM] + [VMEM] * 3,
        out_specs=[VMEM, VMEM],
        out_shape=[
            jax.ShapeDtypeStruct((blocks, 8, BLK), F32),
            jax.ShapeDtypeStruct((4, 6, BLK), F32),
        ],
        compiler_params=pltpu.CompilerParams(vmem_limit_bytes=LIMIT),
        name="nodal",
    )(slot, shared, internal, returned)


def update_kernel(last, *refs):
    if last:
        inverse_ref, force_ref, near_ref, disp_ref, vel_ref, mass_ref, disp_out, vel_out = refs
    else:
        back_ref, ref_ref, inverse_ref, force_ref, near_ref, disp_ref, vel_ref, mass_ref = refs[:8]
        disp_out, vel_out, out_ref, surface = refs[8:]
    blocks = force_ref.shape[0]
    near = [jnp.concatenate([near_ref[s], jnp.zeros((2, BLK), F32)], axis=0) for s in range(4)]
    for k in range(blocks):
        where = slice(k * BLK, (k + 1) * BLK)
        force = force_ref[k]
        for s in range(4):
            entry = jnp.broadcast_to(inverse_ref[s, k : k + 1], (8, BLK))
            force = force + jnp.where(entry >= 0, lanes(near[s], entry & (BLK - 1)), 0.0)
        speed = vel_ref[:, where] + TIME_STEP * mass_ref[:, where] * force[0:6]
        vel_out[:, where] = speed
        disp_out[:, where] = disp_ref[:, where] + TIME_STEP * speed
    if not last:
        pack_blocks(disp_out, ref_ref, None, back_ref, out_ref, surface)


def update(last, back, ref_pos, inverse, force, near, disp, vel, mass):
    outs = [jax.ShapeDtypeStruct(disp.shape, F32)] * 2
    args = (inverse, force, near, disp, vel, mass)
    specs = [VMEM] * 6
    scratch = []
    if not last:
        outs = outs + [jax.ShapeDtypeStruct((back.shape[0], 3, BLK), F32)]
        args = (back, ref_pos) + args
        specs = [SMEM, VMEM] + specs
        scratch = [pltpu.VMEM((force.shape[0] + 1, 8, BLK), F32)]
    return pl.pallas_call(
        functools.partial(update_kernel, last),
        in_specs=specs,
        out_specs=[VMEM] * len(outs),
        out_shape=outs,
        scratch_shapes=scratch,
        compiler_params=pltpu.CompilerParams(vmem_limit_bytes=LIMIT),
        name="update",
    )(*args)


def shift(value, axis, step):
    count = lax.axis_size(axis)
    if step > 0:
        return lax.ppermute(value, axis, [(i, i + 1) for i in range(count - 1)])
    return lax.ppermute(value, axis, [(i + 1, i) for i in range(count - 1)])


def exchange(value):
    return lax.all_to_all(value, ("gx", "gy"), split_axis=0, concat_axis=0, tiled=True)


def body(
    disp,
    vel,
    ref_pos,
    normals,
    mass,
    connectivity,
    stiffness,
    yield_force,
    shared,
    block_slot,
    edge_slots,
    tile_pairs,
    tile_count,
    win_start,
    win_len,
):
    blocks = disp.shape[1] // BLK
    places = lax.axis_size("gx") * lax.axis_size("gy") * CAP
    limit = yield_force.reshape(blocks, BLK)
    match = block_slot[None, :] == jnp.arange(places, dtype=jnp.int32)[:, None]
    back = jnp.min(
        jnp.where(match, jnp.arange(blocks, dtype=jnp.int32)[None, :], blocks), axis=1
    )
    outgoing, inverse = first_pack(back, shared, disp, ref_pos, normals)
    for step in range(STEPS):
        last = step == STEPS - 1
        got = exchange(outgoing)
        if step == 0:
            held_normals = got[:, 3:6]
        else:
            got = jnp.concatenate([got, held_normals], axis=1)
        mine = got[edge_slots]
        edges = jnp.concatenate(
            [shift(mine, "gx", 1), shift(mine, "gx", -1), shift(mine, "gy", 1), shift(mine, "gy", -1)],
            axis=0,
        )
        internal = element_forces(disp, connectivity, stiffness, limit)
        contact = contact_forces(tile_pairs, tile_count, got, edges, win_start, win_len)
        returned = exchange(jnp.transpose(contact, (1, 0, 2)))
        force, sides = nodal_forces(block_slot, shared, internal, returned)
        near = jnp.stack(
            [
                shift(sides[1], "gx", 1),
                shift(sides[0], "gx", -1),
                shift(sides[3], "gy", 1),
                shift(sides[2], "gy", -1),
            ]
        )
        if last:
            disp, vel = update(last, back, ref_pos, inverse, force, near, disp, vel, mass)
        else:
            disp, vel, outgoing = update(last, back, ref_pos, inverse, force, near, disp, vel, mass)
    return disp, vel


def solution(mesh):
    row, flat, lead = P(None, ("gx", "gy")), P(("gx", "gy")), P(("gx", "gy"), None)
    placed = (row, row, row, row, row, row, P(None, None, ("gx", "gy")), flat)
    placed = placed + (row, flat, flat, row, flat, lead, lead)
    return jax.shard_map(
        body, mesh=mesh, in_specs=placed, out_specs=(row, row), check_vma=False
    )
```

```python
import jax
import jax.numpy as jnp
from jax import lax
from jax.experimental import pallas as pl
from jax.experimental.pallas import tpu as pltpu
from jax.sharding import PartitionSpec as P

BLK = 128
CAP = 2
STEPS = 2
TIME_STEP = 0.5
PENALTY = 32.0
THICKNESS = 0.2
F32 = jnp.float32
BF16 = jnp.bfloat16
VMEM = pl.BlockSpec(memory_space=pltpu.VMEM)
SMEM = pl.BlockSpec(memory_space=pltpu.SMEM)
LIMIT = 48 * 1024 * 1024


def rows_iota():
    return lax.broadcasted_iota(jnp.int32, (8, BLK), 0)


def merge_rows(even, odd, bit):
    low = (rows_iota() & bit) == 0
    return jnp.where(low, even, odd) + pltpu.roll(jnp.where(low, odd, even), bit, 0)


def sum_six(parts):
    first = [merge_rows(parts[2 * m], parts[2 * m + 1], 1) for m in range(3)]
    upper = first[2] + pltpu.roll(first[2], 2, 0)
    return merge_rows(merge_rows(first[0], first[1], 2), upper, 4)


def split(value):
    high = value.astype(BF16).astype(F32)
    return high, value - high


def lanes(value, index):
    return jnp.take_along_axis(value, index, axis=1)


def element_block(disp, corner, load_stiff, limit):
    index = jnp.concatenate([corner, corner], axis=0)
    dofs = []
    for pair in range(3):
        source = jnp.concatenate(
            [
                jnp.broadcast_to(disp[2 * pair : 2 * pair + 1], (4, BLK)),
                jnp.broadcast_to(disp[2 * pair + 1 : 2 * pair + 2], (4, BLK)),
            ],
            axis=0,
        )
        dofs.append(lanes(source, index))
    trial = []
    for a in range(4):
        parts = []
        for c in range(6):
            row = load_stiff(4 * c + a).astype(F32)
            parts.append(row[0:8] * dofs[0] + row[8:16] * dofs[1] + row[16:24] * dofs[2])
        trial.append(sum_six(parts))
    squares = trial[0] * trial[0] + trial[1] * trial[1] + trial[2] * trial[2] + trial[3] * trial[3]
    squared = jnp.sum(jnp.where(rows_iota() < 6, squares, 0.0), axis=0, keepdims=True)
    factor = 1.0 / jnp.sqrt(1.0 + squared / (limit * limit))
    node = lax.broadcasted_iota(jnp.int32, (BLK, BLK), 0)
    left = []
    right = []
    for a in range(4):
        high, low = split(trial[a] * factor)
        left.append(jnp.concatenate([high, low], axis=0).astype(BF16))
        right.append(jnp.where(node == corner[a : a + 1], 1.0, 0.0).astype(BF16))
    both = lax.dot_general(
        jnp.concatenate(left, axis=1),
        jnp.concatenate(right, axis=1),
        (((1,), (1,)), ((), ())),
        preferred_element_type=F32,
    )
    return both[0:8] + both[8:16]


def node_table(pos):
    full = jnp.concatenate([pos, pos, jnp.ones((2, BLK), F32)], axis=0)
    high, low = split(full)
    return jnp.concatenate([high, low], axis=0).astype(BF16)


def facet_table(pos, nrm):
    offset = jnp.sum(pos * nrm, axis=0, keepdims=True) + THICKNESS
    nrm_high, nrm_low = split(-nrm)
    off_high, off_low = split(offset)
    half = jnp.concatenate([nrm_high, nrm_low, off_high, off_low], axis=0)
    return jnp.concatenate([half, half], axis=0).astype(BF16)

MESH = pl.DeviceIdType.MESH
NX, NY = 8, 16
DEVICES = NX * NY
PLACES = DEVICES * CAP
CHUNK = 8


def span(block):
    return pl.ds(pl.multiple_of(block * BLK, BLK), BLK)


def partner(order, mx, my):
    def far_first(digit):
        return (0x36 >> (2 * digit)) & 3

    x = ((mx >> 1) + far_first(order >> 5)) & 3
    y = ((my >> 2) + far_first((order >> 3) & 3)) & 3
    z = ((my & 3) + far_first((order >> 1) & 3)) & 3
    return 2 * x + ((mx & 1) ^ (1 - (order & 1))), 4 * y + z


def bytes_wait(ref, sem):
    pltpu.make_async_copy(ref, ref, sem).wait()


def scatter_places(get, out, into, rows, sem_out, sem_in, mx, my):
    me = mx * NY + my

    def one(order, carry):
        px, py = partner(order, mx, my)
        to = px * NY + py
        for q in range(CAP):
            out[CAP * to + q] = get(CAP * to + q)
        pltpu.make_async_remote_copy(
            src_ref=out.at[pl.ds(CAP * to, CAP)],
            dst_ref=into.at[pl.ds(CAP * me, CAP)],
            send_sem=sem_out,
            recv_sem=sem_in,
            device_id=(px, py),
            device_id_type=MESH,
        ).start()
        return carry

    lax.fori_loop(0, DEVICES - 1, one, 0)
    for q in range(CAP):
        into[CAP * me + q] = get(CAP * me + q)


def neighbours(mx, my):
    devices = [
        ((mx + 1) & (NX - 1), my),
        ((mx - 1) & (NX - 1), my),
        (mx, (my + 1) & (NY - 1)),
        (mx, (my - 1) & (NY - 1)),
    ]
    return devices, [mx > 0, mx < NX - 1, my > 0, my < NY - 1]


def send_sides(source, target, sem_out, sem_in, devices):
    for side in range(4):
        pltpu.make_async_remote_copy(
            src_ref=source(side),
            dst_ref=target(side),
            send_sem=sem_out,
            recv_sem=sem_in,
            device_id=devices[side],
            device_id_type=MESH,
        ).start()


def contact_pairs(pairs_ref, start_ref, len_ref, node_tab, facet_tab, tile_out):
    facet = lax.broadcasted_iota(jnp.int32, (BLK, 2 * BLK), 0) << 25
    zero = jnp.zeros((16, BLK), BF16)
    top = jnp.int32(-(2**31))

    def pair(g, carry):
        t = 2 * g
        left = [facet_tab[pairs_ref[1, t + h]] for h in range(2)]
        right = [node_tab[pairs_ref[0, t + h]] for h in range(2)]
        depth = lax.dot_general(
            jnp.concatenate(left, axis=0),
            jnp.concatenate(
                [
                    jnp.concatenate([right[0], zero], axis=1),
                    jnp.concatenate([zero, right[1]], axis=1),
                ],
                axis=0,
            ),
            (((0,), (0,)), ((), ())),
            preferred_element_type=F32,
        )
        start = jnp.concatenate([start_ref[pl.ds(t + h, 1)] for h in range(2)], axis=1)
        length = jnp.concatenate([len_ref[pl.ds(t + h, 1)] for h in range(2)], axis=1)
        shifted = (start << 25) + top
        last = ((length - 1) << 25) + top
        inside = facet - shifted <= last
        pressure = jnp.where(inside, jnp.maximum(depth, 0.0), 0.0)
        high = pressure.astype(BF16)
        low = (pressure - high.astype(F32)).astype(BF16)
        force = lax.dot_general(
            jnp.concatenate(
                [jnp.concatenate([left[h], left[h]], axis=1) for h in range(2)], axis=0
            ),
            jnp.concatenate([high, low], axis=0),
            (((1,), (0,)), ((), ())),
            preferred_element_type=F32,
        )
        tile_out[pl.ds(pl.multiple_of(8 * t, 16), 8)] = force[0:8, 0:BLK]
        tile_out[pl.ds(pl.multiple_of(8 * t + 8, 8), 8)] = force[16:24, BLK : 2 * BLK]
        return carry

    lax.fori_loop(0, start_ref.shape[0] // 2, pair, 0, unroll=16)


def place_sums(count_ref, slave_ref, tile_out, box):
    tiles = slave_ref.shape[1]
    place = lax.broadcasted_iota(jnp.int32, (PLACES, tiles), 0)
    active = lax.broadcasted_iota(jnp.int32, (PLACES, tiles), 1) < count_ref[0]
    pick = jnp.where((place == slave_ref[...]) & active, -PENALTY / BLK, 0.0).astype(BF16)
    for c in range(3):
        total = tile_out[pl.ds(c, tiles, 8)] + tile_out[pl.ds(c + 3, tiles, 8)]
        high, low = split(total)
        both = jnp.dot(
            pick,
            jnp.concatenate([high.astype(BF16), low.astype(BF16)], axis=1),
            preferred_element_type=F32,
        )
        box[pl.ds(c, PLACES, 8)] = both[:, 0:BLK] + both[:, BLK : 2 * BLK]


def invert_lists(shared_ref, inverse):
    blocks = inverse.shape[1]
    block = lax.broadcasted_iota(jnp.int32, (blocks, BLK), 0)
    entry = (lax.broadcasted_iota(jnp.int32, (blocks, BLK), 1) + 1).astype(F32)
    lane = lax.broadcasted_iota(jnp.int32, (BLK, BLK), 0)
    for side in range(4):
        node = shared_ref[side : side + 1]
        found = lax.dot_general(
            jnp.where(block == (node >> 7), entry, 0.0).astype(BF16),
            jnp.where(lane == (node & (BLK - 1)), 1.0, 0.0).astype(BF16),
            (((1,), (1,)), ((), ())),
            preferred_element_type=F32,
        )
        inverse[side] = found.astype(jnp.int32) - 1


def crash_kernel(
    back_ref,
    slot_ref,
    edge_ref,
    pairs_ref,
    count_ref,
    disp_in,
    vel_in,
    ref_ref,
    nrm_ref,
    mass_ref,
    corner_ref,
    stiff_hbm,
    limit_ref,
    shared_ref,
    slave_ref,
    start_ref,
    len_ref,
    disp_ref,
    vel_ref,
    stiff,
    surface,
    out6,
    got6,
    out3,
    got3,
    edge_out6,
    edge_in6,
    edge_out3,
    edge_in3,
    node_tab,
    facet_tab,
    tile_out,
    box,
    home_out,
    home,
    internal,
    force,
    side_out,
    near,
    inverse,
    stiff_sem,
    sem_out,
    sem_in,
):
    mx, my = lax.axis_index("gx"), lax.axis_index("gy")
    blocks = internal.shape[0]
    edges = edge_out3.shape[0]
    devices, exists = neighbours(mx, my)

    def stiff_copy(chunk):
        where = pl.ds(pl.multiple_of(chunk * CHUNK * BLK, BLK), CHUNK * BLK)
        return pltpu.make_async_copy(
            stiff_hbm.at[:, :, where], stiff.at[:, :, where], stiff_sem.at[chunk]
        )

    barrier = pltpu.get_barrier_semaphore()

    def greet(order, carry):
        pl.semaphore_signal(
            barrier, inc=1, device_id=partner(order, mx, my), device_id_type=MESH
        )
        return carry

    lax.fori_loop(0, DEVICES - 1, greet, 0)
    for chunk in range(blocks // CHUNK):
        stiff_copy(chunk).start()
    invert_lists(shared_ref, inverse)
    surface[blocks] = jnp.zeros((8, BLK), F32)

    def first_surface(k, carry):
        where = span(k)
        surface[k, 0:3] = ref_ref[:, where] + disp_in[0:3, where]
        surface[k, 3:6] = nrm_ref[:, where]
        return carry

    lax.fori_loop(0, blocks, first_surface, 0, unroll=8)
    pl.semaphore_wait(barrier, DEVICES - 1)

    for step in range(STEPS):
        disp, vel = (disp_in, vel_in) if step == 0 else (disp_ref, vel_ref)
        out, got = (out6, got6) if step == 0 else (out3, got3)
        edge_out, edge_in = (edge_out6, edge_in6) if step == 0 else (edge_out3, edge_in3)
        rows = 6 if step == 0 else 3
        phase = 4 * step
        scatter_places(
            lambda r: surface[back_ref[r]][0:rows],
            out,
            got,
            rows,
            sem_out.at[phase],
            sem_in.at[phase],
            mx,
            my,
        )

        def elements(k, carry):
            where = span(k)
            internal[k] = element_block(
                disp[:, where],
                corner_ref[:, where] & (BLK - 1),
                lambda i: stiff[i, :, where],
                limit_ref[pl.ds(k, 1)],
            )
            return carry

        for chunk in range(blocks // CHUNK):
            if step == 0:
                stiff_copy(chunk).wait()
        lax.fori_loop(0, blocks, elements, 0, unroll=4)

        bytes_wait(got.at[pl.ds(0, PLACES - CAP)], sem_in.at[phase])
        for e in range(edges):
            edge_out[e] = got[edge_ref[e]]
        send_sides(
            lambda side: edge_out,
            lambda side: edge_in.at[pl.ds(edges * side, edges)],
            sem_out.at[phase + 1],
            sem_in.at[phase + 1],
            devices,
        )

        def tables(r, carry):
            pos = got[r][0:3]
            node_tab[r] = node_table(pos)
            facet_tab[r] = facet_table(pos, got6[r][3:6])
            return carry

        lax.fori_loop(0, PLACES, tables, 0, unroll=4)
        bytes_wait(edge_in, sem_in.at[phase + 1])
        for side in range(4):
            for e in range(edges):
                at = edges * side + e
                pos = jnp.where(exists[side], edge_in[at][0:3], 0.0)
                nrm = jnp.where(exists[side], edge_in6[at][3:6], 0.0)
                facet_tab[PLACES + at] = facet_table(pos, nrm)
        contact_pairs(pairs_ref, start_ref, len_ref, node_tab, facet_tab, tile_out)
        place_sums(count_ref, slave_ref, tile_out, box)
        scatter_places(
            lambda r: box[pl.ds(pl.multiple_of(8 * r, 8), 8)][0:3],
            home_out.at[step],
            home.at[step],
            3,
            sem_out.at[phase + 2],
            sem_in.at[phase + 2],
            mx,
            my,
        )
        bytes_wait(home.at[step, pl.ds(0, PLACES - CAP)], sem_in.at[phase + 2])

        node = [jnp.broadcast_to(shared_ref[s : s + 1], (8, BLK)) for s in range(4)]
        none = jnp.zeros((5, BLK), F32)

        def nodal(k, found):
            contact = jnp.concatenate([home[step, slot_ref[k]], none], axis=0)
            total = contact - internal[k]
            force[k] = total
            return tuple(
                jnp.where((node[s] >> 7) == k, lanes(total, node[s] & (BLK - 1)), found[s])
                for s in range(4)
            )

        found = lax.fori_loop(
            0, blocks, nodal, tuple(jnp.zeros((8, BLK), F32) for s in range(4)), unroll=8
        )
        for s in range(4):
            side_out[step, s] = found[s][0:6]
        give = (1, 0, 3, 2)
        send_sides(
            lambda side: side_out.at[step, give[side]],
            lambda side: near.at[step, side],
            sem_out.at[phase + 3],
            sem_in.at[phase + 3],
            devices,
        )

        def advance(k, carry):
            where = span(k)
            vel_ref[:, where] = vel[:, where] + TIME_STEP * mass_ref[:, where] * force[k][0:6]
            return carry

        lax.fori_loop(0, blocks, advance, 0, unroll=8)
        bytes_wait(near.at[step], sem_in.at[phase + 3])
        given = [
            jnp.concatenate(
                [jnp.where(exists[s], near[step, s], 0.0), jnp.zeros((2, BLK), F32)], axis=0
            )
            for s in range(4)
        ]

        def assemble(k, carry):
            where = span(k)
            added = jnp.zeros((8, BLK), F32)
            for s in range(4):
                entry = jnp.broadcast_to(inverse[s, pl.ds(k, 1)], (8, BLK))
                added = added + jnp.where(entry >= 0, lanes(given[s], entry & (BLK - 1)), 0.0)
            speed = vel_ref[:, where] + TIME_STEP * mass_ref[:, where] * added[0:6]
            moved = disp[:, where] + TIME_STEP * speed
            vel_ref[:, where] = speed
            disp_ref[:, where] = moved
            if step < STEPS - 1:
                surface[k, 0:3] = ref_ref[:, where] + moved[0:3]
            return carry

        lax.fori_loop(0, blocks, assemble, 0, unroll=8)

    for step in range(STEPS):
        phase = 4 * step
        out = out6 if step == 0 else out3
        edge_in = edge_in6 if step == 0 else edge_in3
        bytes_wait(out.at[pl.ds(0, PLACES - CAP)], sem_out.at[phase])
        bytes_wait(edge_in, sem_out.at[phase + 1])
        bytes_wait(home_out.at[step, pl.ds(0, PLACES - CAP)], sem_out.at[phase + 2])
        bytes_wait(near.at[step], sem_out.at[phase + 3])


def body(
    disp,
    vel,
    ref_pos,
    normals,
    mass,
    connectivity,
    stiffness,
    yield_force,
    shared,
    block_slot,
    edge_slots,
    tile_pairs,
    tile_count,
    win_start,
    win_len,
):
    blocks = disp.shape[1] // BLK
    tiles = win_start.shape[0]
    edges = edge_slots.shape[0]
    limit = yield_force.reshape(blocks, BLK)
    match = block_slot[None, :] == jnp.arange(PLACES, dtype=jnp.int32)[:, None]
    back = jnp.min(
        jnp.where(match, jnp.arange(blocks, dtype=jnp.int32)[None, :], blocks), axis=1
    )

    def vmem(*shape):
        return pltpu.VMEM(shape, F32)

    return pl.pallas_call(
        crash_kernel,
        in_specs=[SMEM] * 5 + [VMEM] * 6 + [pl.BlockSpec(memory_space=pl.ANY)] + [VMEM] * 5,
        out_specs=[VMEM, VMEM],
        out_shape=[jax.ShapeDtypeStruct(disp.shape, F32)] * 2,
        scratch_shapes=[
            pltpu.VMEM(stiffness.shape, BF16),
            vmem(blocks + 1, 8, BLK),
            vmem(PLACES, 6, BLK),
            vmem(PLACES, 6, BLK),
            vmem(PLACES, 3, BLK),
            vmem(PLACES, 3, BLK),
            vmem(edges, 6, BLK),
            vmem(4 * edges, 6, BLK),
            vmem(edges, 3, BLK),
            vmem(4 * edges, 3, BLK),
            pltpu.VMEM((PLACES, 16, BLK), BF16),
            pltpu.VMEM((PLACES + 4 * edges, 16, BLK), BF16),
            vmem(8 * tiles, BLK),
            vmem(8 * PLACES, BLK),
            vmem(STEPS, PLACES, 3, BLK),
            vmem(STEPS, PLACES, 3, BLK),
            vmem(blocks, 8, BLK),
            vmem(blocks, 8, BLK),
            vmem(STEPS, 4, 6, BLK),
            vmem(STEPS, 4, 6, BLK),
            pltpu.VMEM((4, blocks, BLK), jnp.int32),
            pltpu.SemaphoreType.DMA((blocks // CHUNK,)),
            pltpu.SemaphoreType.DMA((4 * STEPS,)),
            pltpu.SemaphoreType.DMA((4 * STEPS,)),
        ],
        compiler_params=pltpu.CompilerParams(
            vmem_limit_bytes=LIMIT, collective_id=0, has_side_effects=True
        ),
        name="crash_steps",
    )(
        back,
        block_slot,
        edge_slots,
        tile_pairs,
        tile_count,
        disp,
        vel,
        ref_pos,
        normals,
        mass,
        connectivity,
        stiffness,
        limit,
        shared,
        tile_pairs[0:1],
        win_start,
        win_len,
    )


def solution(mesh):
    row, flat, lead = P(None, ("gx", "gy")), P(("gx", "gy")), P(("gx", "gy"), None)
    placed = (row, row, row, row, row, row, P(None, None, ("gx", "gy")), flat)
    placed = placed + (row, flat, flat, row, flat, lead, lead)
    return jax.shard_map(
        body, mesh=mesh, in_specs=placed, out_specs=(row, row), check_vma=False
    )
```

```python
import jax
import jax.numpy as jnp
from jax import lax
from jax.experimental import pallas as pl
from jax.experimental.pallas import tpu as pltpu
from jax.sharding import PartitionSpec as P

BLK = 128
CAP = 2
STEPS = 2
TIME_STEP = 0.5
PENALTY = 32.0
THICKNESS = 0.2
F32 = jnp.float32
BF16 = jnp.bfloat16
VMEM = pl.BlockSpec(memory_space=pltpu.VMEM)
SMEM = pl.BlockSpec(memory_space=pltpu.SMEM)
LIMIT = 64 * 1024 * 1024 - 65536


def rows_iota():
    return lax.broadcasted_iota(jnp.int32, (8, BLK), 0)


def merge_rows(even, odd, bit):
    low = (rows_iota() & bit) == 0
    return jnp.where(low, even, odd) + pltpu.roll(jnp.where(low, odd, even), bit, 0)


def sum_six(parts):
    first = [merge_rows(parts[2 * m], parts[2 * m + 1], 1) for m in range(3)]
    upper = first[2] + pltpu.roll(first[2], 2, 0)
    return merge_rows(merge_rows(first[0], first[1], 2), upper, 4)


def split(value):
    high = value.astype(BF16).astype(F32)
    return high, value - high


def lanes(value, index):
    return jnp.take_along_axis(value, index, axis=1)


def element_block(disp, corner, load_stiff, limit):
    index = jnp.concatenate([corner, corner], axis=0)
    dofs = []
    for pair in range(3):
        source = jnp.concatenate(
            [
                jnp.broadcast_to(disp[2 * pair : 2 * pair + 1], (4, BLK)),
                jnp.broadcast_to(disp[2 * pair + 1 : 2 * pair + 2], (4, BLK)),
            ],
            axis=0,
        )
        dofs.append(lanes(source, index))
    trial = []
    for a in range(4):
        parts = []
        for c in range(6):
            row = load_stiff(4 * c + a).astype(F32)
            parts.append(row[0:8] * dofs[0] + row[8:16] * dofs[1] + row[16:24] * dofs[2])
        trial.append(sum_six(parts))
    squares = trial[0] * trial[0] + trial[1] * trial[1] + trial[2] * trial[2] + trial[3] * trial[3]
    squared = jnp.sum(jnp.where(rows_iota() < 6, squares, 0.0), axis=0, keepdims=True)
    factor = 1.0 / jnp.sqrt(1.0 + squared / (limit * limit))
    node = lax.broadcasted_iota(jnp.int32, (BLK, BLK), 0)
    left = []
    right = []
    for a in range(4):
        high, low = split(trial[a] * factor)
        left.append(jnp.concatenate([high, low], axis=0).astype(BF16))
        right.append(jnp.where(node == corner[a : a + 1], 1.0, 0.0).astype(BF16))
    both = lax.dot_general(
        jnp.concatenate(left, axis=1),
        jnp.concatenate(right, axis=1),
        (((1,), (1,)), ((), ())),
        preferred_element_type=F32,
    )
    return both[0:8] + both[8:16]


def node_table(pos):
    full = jnp.concatenate([pos, pos, jnp.ones((2, BLK), F32)], axis=0)
    high, low = split(full)
    return jnp.concatenate([high, low], axis=0).astype(BF16)


def facet_table(pos, nrm):
    offset = jnp.sum(pos * nrm, axis=0, keepdims=True) + THICKNESS
    nrm_high, nrm_low = split(-nrm)
    off_high, off_low = split(offset)
    half = jnp.concatenate([nrm_high, nrm_low, off_high, off_low], axis=0)
    return jnp.concatenate([half, half], axis=0).astype(BF16)

MESH = pl.DeviceIdType.MESH
NX, NY = 8, 16
DEVICES = NX * NY
PLACES = DEVICES * CAP
CHUNK = 8
GREET = 8
SENDS = 127
EARLY = (64, 32)
PAIRS = 32
BODY = 8


def span(block):
    return pl.ds(pl.multiple_of(block * BLK, BLK), BLK)


def partner(order, mx, my):
    def far_first(digit):
        return (0x36 >> (2 * digit)) & 3

    x = ((mx >> 1) + far_first(order >> 5)) & 3
    y = ((my >> 2) + far_first((order >> 3) & 3)) & 3
    z = ((my & 3) + far_first((order >> 1) & 3)) & 3
    return 2 * x + ((mx & 1) ^ (1 - (order & 1))), 4 * y + z


def bytes_wait(ref, sem):
    pltpu.make_async_copy(ref, ref, sem).wait()


def scatter_places(get, out, into, rows, sem_out, sem_in, mx, my):
    me = mx * NY + my

    def one(order, carry):
        px, py = partner(order, mx, my)
        to = px * NY + py
        for q in range(CAP):
            out[CAP * to + q] = get(CAP * to + q)
        pltpu.make_async_remote_copy(
            src_ref=out.at[pl.ds(CAP * to, CAP)],
            dst_ref=into.at[pl.ds(CAP * me, CAP)],
            send_sem=sem_out,
            recv_sem=sem_in,
            device_id=(px, py),
            device_id_type=MESH,
        ).start()
        return carry

    lax.fori_loop(0, DEVICES - 1, one, 0, unroll=SENDS)
    for q in range(CAP):
        into[CAP * me + q] = get(CAP * me + q)


def neighbours(mx, my):
    devices = [
        ((mx + 1) & (NX - 1), my),
        ((mx - 1) & (NX - 1), my),
        (mx, (my + 1) & (NY - 1)),
        (mx, (my - 1) & (NY - 1)),
    ]
    return devices, [mx > 0, mx < NX - 1, my > 0, my < NY - 1]


def send_sides(source, target, sem_out, sem_in, devices):
    for side in range(4):
        pltpu.make_async_remote_copy(
            src_ref=source(side),
            dst_ref=target(side),
            send_sem=sem_out,
            recv_sem=sem_in,
            device_id=devices[side],
            device_id_type=MESH,
        ).start()


def contact_pairs(pairs_ref, start_ref, len_ref, node_tab, facet_tab, tile_out):
    facet = lax.broadcasted_iota(jnp.int32, (BLK, 2 * BLK), 0) << 25
    zero = jnp.zeros((16, BLK), BF16)
    top = jnp.int32(-(2**31))

    def pair(g, carry):
        t = 2 * g
        left = [facet_tab[pairs_ref[1, t + h]] for h in range(2)]
        right = [node_tab[pairs_ref[0, t + h]] for h in range(2)]
        depth = lax.dot_general(
            jnp.concatenate(left, axis=0),
            jnp.concatenate(
                [
                    jnp.concatenate([right[0], zero], axis=1),
                    jnp.concatenate([zero, right[1]], axis=1),
                ],
                axis=0,
            ),
            (((0,), (0,)), ((), ())),
            preferred_element_type=F32,
        )
        start = jnp.concatenate([start_ref[pl.ds(t + h, 1)] for h in range(2)], axis=1)
        length = jnp.concatenate([len_ref[pl.ds(t + h, 1)] for h in range(2)], axis=1)
        shifted = (start << 25) + top
        last = ((length - 1) << 25) + top
        inside = facet - shifted <= last
        pressure = jnp.where(inside, jnp.maximum(depth, 0.0), 0.0)
        high = pressure.astype(BF16)
        low = (pressure - high.astype(F32)).astype(BF16)
        force = lax.dot_general(
            jnp.concatenate(
                [jnp.concatenate([left[h], left[h]], axis=1) for h in range(2)], axis=0
            ),
            jnp.concatenate([high, low], axis=0),
            (((1,), (0,)), ((), ())),
            preferred_element_type=F32,
        )
        tile_out[pl.ds(pl.multiple_of(8 * t, 16), 8)] = force[0:8, 0:BLK]
        tile_out[pl.ds(pl.multiple_of(8 * t + 8, 8), 8)] = force[16:24, BLK : 2 * BLK]
        return carry

    lax.fori_loop(0, start_ref.shape[0] // 2, pair, 0, unroll=PAIRS)


def place_sums(count_ref, slave_ref, tile_out, box):
    tiles = slave_ref.shape[1]
    place = lax.broadcasted_iota(jnp.int32, (PLACES, tiles), 0)
    active = lax.broadcasted_iota(jnp.int32, (PLACES, tiles), 1) < count_ref[0]
    pick = jnp.where((place == slave_ref[0:1]) & active, -PENALTY / BLK, 0.0).astype(BF16)
    for c in range(3):
        total = tile_out[pl.ds(c, tiles, 8)] + tile_out[pl.ds(c + 3, tiles, 8)]
        high, low = split(total)
        both = jnp.dot(
            pick,
            jnp.concatenate([high.astype(BF16), low.astype(BF16)], axis=1),
            preferred_element_type=F32,
        )
        box[pl.ds(c, PLACES, 8)] = both[:, 0:BLK] + both[:, BLK : 2 * BLK]


def invert_lists(shared_ref, inverse):
    blocks = inverse.shape[1]
    block = lax.broadcasted_iota(jnp.int32, (blocks, BLK), 0)
    entry = (lax.broadcasted_iota(jnp.int32, (blocks, BLK), 1) + 1).astype(F32)
    lane = lax.broadcasted_iota(jnp.int32, (BLK, BLK), 0)
    for side in range(4):
        node = shared_ref[side : side + 1]
        found = lax.dot_general(
            jnp.where(block == (node >> 7), entry, 0.0).astype(BF16),
            jnp.where(lane == (node & (BLK - 1)), 1.0, 0.0).astype(BF16),
            (((1,), (1,)), ((), ())),
            preferred_element_type=F32,
        )
        inverse[side] = found.astype(jnp.int32) - 1


def crash_kernel(
    back_ref,
    slot_ref,
    edge_ref,
    pairs_ref,
    count_ref,
    disp_hbm,
    vel_hbm,
    ref_hbm,
    nrm_hbm,
    mass_hbm,
    corner_hbm,
    stiff_hbm,
    limit_hbm,
    shared_hbm,
    slave_hbm,
    start_hbm,
    len_hbm,
    disp_ref,
    vel_ref,
    disp_in,
    vel_in,
    ref_ref,
    nrm_ref,
    mass_ref,
    corner_ref,
    limit_ref,
    shared_ref,
    slave_ref,
    start_ref,
    len_ref,
    stiff,
    surface,
    out6,
    got6,
    out3,
    got3,
    edge_out6,
    edge_in6,
    edge_out3,
    edge_in3,
    node_tab,
    facet_tab,
    tile_out,
    box,
    home_out,
    home,
    internal,
    force,
    side_out,
    near,
    inverse,
    load_sem,
    stiff_sem,
    sem_out,
    sem_in,
):
    mx, my = lax.axis_index("gx"), lax.axis_index("gy")
    blocks = internal.shape[0]
    edges = edge_out3.shape[0]
    devices, exists = neighbours(mx, my)

    def stiff_copy(chunk):
        where = pl.ds(pl.multiple_of(chunk * CHUNK * BLK, BLK), CHUNK * BLK)
        return pltpu.make_async_copy(
            stiff_hbm.at[:, :, where], stiff.at[:, :, where], stiff_sem.at[chunk]
        )

    loads = [
        pltpu.make_async_copy(source, target, load_sem.at[i])
        for i, (source, target) in enumerate(
            (
                (disp_hbm, disp_in),
                (ref_hbm, ref_ref),
                (nrm_hbm, nrm_ref),
                (shared_hbm, shared_ref),
                (corner_hbm, corner_ref),
                (limit_hbm, limit_ref),
                (vel_hbm, vel_in),
                (mass_hbm, mass_ref),
                (slave_hbm, slave_ref),
                (start_hbm, start_ref),
                (len_hbm, len_ref),
            )
        )
    ]
    for load in loads:
        load.start()
    barrier = pltpu.get_barrier_semaphore()

    def greet(order, carry):
        pl.semaphore_signal(
            barrier, inc=1, device_id=partner(order, mx, my), device_id_type=MESH
        )
        return carry

    lax.fori_loop(0, DEVICES - 1, greet, 0, unroll=GREET)
    for chunk in range(blocks // CHUNK):
        stiff_copy(chunk).start()
    for load in loads[0:4]:
        load.wait()
    invert_lists(shared_ref, inverse)
    surface[blocks] = jnp.zeros((8, BLK), F32)

    def first_surface(k, carry):
        where = span(k)
        surface[k, 0:3] = ref_ref[:, where] + disp_in[0:3, where]
        surface[k, 3:6] = nrm_ref[:, where]
        return carry

    lax.fori_loop(0, blocks, first_surface, 0, unroll=8)
    pl.semaphore_wait(barrier, DEVICES - 1)

    for step in range(STEPS):
        disp, vel = (disp_in, vel_in) if step == 0 else (disp_ref, vel_ref)
        out, got = (out6, got6) if step == 0 else (out3, got3)
        edge_out, edge_in = (edge_out6, edge_in6) if step == 0 else (edge_out3, edge_in3)
        rows = 6 if step == 0 else 3
        phase = 4 * step
        scatter_places(
            lambda r: surface[back_ref[r]][0:rows],
            out,
            got,
            rows,
            sem_out.at[phase],
            sem_in.at[phase],
            mx,
            my,
        )

        def elements(k, carry):
            where = span(k)
            internal[k] = element_block(
                disp[:, where],
                corner_ref[:, where] & (BLK - 1),
                lambda i: stiff[i, :, where],
                limit_ref[pl.ds(k, 1)],
            )
            return carry

        if step == 0:
            for load in loads[4:]:
                load.wait()
            for chunk in range(blocks // CHUNK):
                stiff_copy(chunk).wait()
        lax.fori_loop(0, EARLY[step], elements, 0, unroll=BODY)

        bytes_wait(got.at[pl.ds(0, PLACES - CAP)], sem_in.at[phase])
        for e in range(edges):
            edge_out[e] = got[edge_ref[e]]
        send_sides(
            lambda side: edge_out,
            lambda side: edge_in.at[pl.ds(edges * side, edges)],
            sem_out.at[phase + 1],
            sem_in.at[phase + 1],
            devices,
        )

        def tables(r, carry):
            pos = got[r][0:3]
            node_tab[r] = node_table(pos)
            facet_tab[r] = facet_table(pos, got6[r][3:6])
            return carry

        lax.fori_loop(0, PLACES, tables, 0, unroll=4)
        bytes_wait(edge_in, sem_in.at[phase + 1])
        for side in range(4):
            for e in range(edges):
                at = edges * side + e
                pos = jnp.where(exists[side], edge_in[at][0:3], 0.0)
                nrm = jnp.where(exists[side], edge_in6[at][3:6], 0.0)
                facet_tab[PLACES + at] = facet_table(pos, nrm)
        contact_pairs(pairs_ref, start_ref, len_ref, node_tab, facet_tab, tile_out)
        place_sums(count_ref, slave_ref, tile_out, box)
        scatter_places(
            lambda r: box[pl.ds(pl.multiple_of(8 * r, 8), 8)][0:3],
            home_out.at[step],
            home.at[step],
            3,
            sem_out.at[phase + 2],
            sem_in.at[phase + 2],
            mx,
            my,
        )
        lax.fori_loop(EARLY[step], blocks, elements, 0, unroll=BODY)
        bytes_wait(home.at[step, pl.ds(0, PLACES - CAP)], sem_in.at[phase + 2])

        node = [jnp.broadcast_to(shared_ref[s : s + 1], (8, BLK)) for s in range(4)]
        none = jnp.zeros((5, BLK), F32)

        def nodal(k, found):
            contact = jnp.concatenate([home[step, slot_ref[k]], none], axis=0)
            total = contact - internal[k]
            force[k] = total
            return tuple(
                jnp.where((node[s] >> 7) == k, lanes(total, node[s] & (BLK - 1)), found[s])
                for s in range(4)
            )

        found = lax.fori_loop(
            0, blocks, nodal, tuple(jnp.zeros((8, BLK), F32) for s in range(4)), unroll=8
        )
        for s in range(4):
            side_out[step, s] = found[s][0:6]
        give = (1, 0, 3, 2)
        send_sides(
            lambda side: side_out.at[step, give[side]],
            lambda side: near.at[step, side],
            sem_out.at[phase + 3],
            sem_in.at[phase + 3],
            devices,
        )

        def advance(k, carry):
            where = span(k)
            vel_ref[:, where] = vel[:, where] + TIME_STEP * mass_ref[:, where] * force[k][0:6]
            return carry

        lax.fori_loop(0, blocks, advance, 0, unroll=8)
        bytes_wait(near.at[step], sem_in.at[phase + 3])
        given = [
            jnp.concatenate(
                [jnp.where(exists[s], near[step, s], 0.0), jnp.zeros((2, BLK), F32)], axis=0
            )
            for s in range(4)
        ]

        def assemble(k, carry):
            where = span(k)
            added = jnp.zeros((8, BLK), F32)
            for s in range(4):
                entry = jnp.broadcast_to(inverse[s, pl.ds(k, 1)], (8, BLK))
                added = added + jnp.where(entry >= 0, lanes(given[s], entry & (BLK - 1)), 0.0)
            speed = vel_ref[:, where] + TIME_STEP * mass_ref[:, where] * added[0:6]
            moved = disp[:, where] + TIME_STEP * speed
            vel_ref[:, where] = speed
            disp_ref[:, where] = moved
            if step < STEPS - 1:
                surface[k, 0:3] = ref_ref[:, where] + moved[0:3]
            return carry

        lax.fori_loop(0, blocks, assemble, 0, unroll=8)

    for step in range(STEPS):
        phase = 4 * step
        out = out6 if step == 0 else out3
        edge_in = edge_in6 if step == 0 else edge_in3
        bytes_wait(out.at[pl.ds(0, PLACES - CAP)], sem_out.at[phase])
        bytes_wait(edge_in, sem_out.at[phase + 1])
        bytes_wait(home_out.at[step, pl.ds(0, PLACES - CAP)], sem_out.at[phase + 2])
        bytes_wait(near.at[step], sem_out.at[phase + 3])


def body(
    disp,
    vel,
    ref_pos,
    normals,
    mass,
    connectivity,
    stiffness,
    yield_force,
    shared,
    block_slot,
    edge_slots,
    tile_pairs,
    tile_count,
    win_start,
    win_len,
):
    blocks = disp.shape[1] // BLK
    tiles = win_start.shape[0]
    edges = edge_slots.shape[0]
    limit = yield_force.reshape(blocks, BLK)
    match = block_slot[None, :] == jnp.arange(PLACES, dtype=jnp.int32)[:, None]
    back = jnp.min(
        jnp.where(match, jnp.arange(blocks, dtype=jnp.int32)[None, :], blocks), axis=1
    )

    def vmem(*shape):
        return pltpu.VMEM(shape, F32)

    return pl.pallas_call(
        crash_kernel,
        in_specs=[SMEM] * 5 + [pl.BlockSpec(memory_space=pl.ANY)] * 12,
        out_specs=[VMEM, VMEM],
        out_shape=[jax.ShapeDtypeStruct(disp.shape, F32)] * 2,
        scratch_shapes=[
            vmem(*disp.shape),
            vmem(*vel.shape),
            vmem(*ref_pos.shape),
            vmem(*normals.shape),
            vmem(*mass.shape),
            pltpu.VMEM(connectivity.shape, jnp.int32),
            vmem(*limit.shape),
            pltpu.VMEM(shared.shape, jnp.int32),
            pltpu.VMEM(tile_pairs.shape, jnp.int32),
            pltpu.VMEM(win_start.shape, jnp.int32),
            pltpu.VMEM(win_len.shape, jnp.int32),
            pltpu.VMEM(stiffness.shape, BF16),
            vmem(blocks + 1, 8, BLK),
            vmem(PLACES, 6, BLK),
            vmem(PLACES, 6, BLK),
            vmem(PLACES, 3, BLK),
            vmem(PLACES, 3, BLK),
            vmem(edges, 6, BLK),
            vmem(4 * edges, 6, BLK),
            vmem(edges, 3, BLK),
            vmem(4 * edges, 3, BLK),
            pltpu.VMEM((PLACES, 16, BLK), BF16),
            pltpu.VMEM((PLACES + 4 * edges, 16, BLK), BF16),
            vmem(8 * tiles, BLK),
            vmem(8 * PLACES, BLK),
            vmem(STEPS, PLACES, 3, BLK),
            vmem(STEPS, PLACES, 3, BLK),
            vmem(blocks, 8, BLK),
            vmem(blocks, 8, BLK),
            vmem(STEPS, 4, 6, BLK),
            vmem(STEPS, 4, 6, BLK),
            pltpu.VMEM((4, blocks, BLK), jnp.int32),
            pltpu.SemaphoreType.DMA((11,)),
            pltpu.SemaphoreType.DMA((blocks // CHUNK,)),
            pltpu.SemaphoreType.DMA((4 * STEPS,)),
            pltpu.SemaphoreType.DMA((4 * STEPS,)),
        ],
        compiler_params=pltpu.CompilerParams(
            vmem_limit_bytes=LIMIT, collective_id=0, has_side_effects=True
        ),
        name="crash_steps",
    )(
        back,
        block_slot,
        edge_slots,
        tile_pairs,
        tile_count,
        disp,
        vel,
        ref_pos,
        normals,
        mass,
        connectivity,
        stiffness,
        limit,
        shared,
        tile_pairs,
        win_start,
        win_len,
    )


def solution(mesh):
    row, flat, lead = P(None, ("gx", "gy")), P(("gx", "gy")), P(("gx", "gy"), None)
    placed = (row, row, row, row, row, row, P(None, None, ("gx", "gy")), flat)
    placed = placed + (row, flat, flat, row, flat, lead, lead)
    return jax.shard_map(
        body, mesh=mesh, in_specs=placed, out_specs=(row, row), check_vma=False
    )
```

```python
import jax
import jax.numpy as jnp
from jax import lax
from jax.experimental import pallas as pl
from jax.experimental.pallas import tpu as pltpu
from jax.sharding import PartitionSpec as P

BLK = 128
CAP = 2
STEPS = 2
TIME_STEP = 0.5
PENALTY = 32.0
THICKNESS = 0.2
F32 = jnp.float32
BF16 = jnp.bfloat16
VMEM = pl.BlockSpec(memory_space=pltpu.VMEM)
SMEM = pl.BlockSpec(memory_space=pltpu.SMEM)
LIMIT = 64 * 1024 * 1024 - 65536


def rows_iota():
    return lax.broadcasted_iota(jnp.int32, (8, BLK), 0)


def merge_rows(even, odd, bit):
    low = (rows_iota() & bit) == 0
    return jnp.where(low, even, odd) + pltpu.roll(jnp.where(low, odd, even), bit, 0)


def sum_six(parts):
    first = [merge_rows(parts[2 * m], parts[2 * m + 1], 1) for m in range(3)]
    upper = first[2] + pltpu.roll(first[2], 2, 0)
    return merge_rows(merge_rows(first[0], first[1], 2), upper, 4)


def split(value):
    high = value.astype(BF16).astype(F32)
    return high, value - high


def lanes(value, index):
    return jnp.take_along_axis(value, index, axis=1)


def element_block(disp, corner, load_stiff, limit):
    index = jnp.concatenate([corner, corner], axis=0)
    dofs = []
    for pair in range(3):
        source = jnp.concatenate(
            [
                jnp.broadcast_to(disp[2 * pair : 2 * pair + 1], (4, BLK)),
                jnp.broadcast_to(disp[2 * pair + 1 : 2 * pair + 2], (4, BLK)),
            ],
            axis=0,
        )
        dofs.append(lanes(source, index))
    trial = []
    for a in range(4):
        parts = []
        for c in range(6):
            row = load_stiff(4 * c + a).astype(F32)
            parts.append(row[0:8] * dofs[0] + row[8:16] * dofs[1] + row[16:24] * dofs[2])
        trial.append(sum_six(parts))
    squares = trial[0] * trial[0] + trial[1] * trial[1] + trial[2] * trial[2] + trial[3] * trial[3]
    squared = jnp.sum(jnp.where(rows_iota() < 6, squares, 0.0), axis=0, keepdims=True)
    factor = 1.0 / jnp.sqrt(1.0 + squared / (limit * limit))
    node = lax.broadcasted_iota(jnp.int32, (BLK, BLK), 0)
    left = []
    right = []
    for a in range(4):
        high, low = split(trial[a] * factor)
        left.append(jnp.concatenate([high, low], axis=0).astype(BF16))
        right.append(jnp.where(node == corner[a : a + 1], 1.0, 0.0).astype(BF16))
    both = lax.dot_general(
        jnp.concatenate(left, axis=1),
        jnp.concatenate(right, axis=1),
        (((1,), (1,)), ((), ())),
        preferred_element_type=F32,
    )
    return both[0:8] + both[8:16]


def node_table(pos):
    full = jnp.concatenate([pos, pos, jnp.ones((2, BLK), F32)], axis=0)
    high, low = split(full)
    return jnp.concatenate([high, low], axis=0).astype(BF16)


def facet_table(pos, nrm):
    offset = jnp.sum(pos * nrm, axis=0, keepdims=True) + THICKNESS
    nrm_high, nrm_low = split(-nrm)
    off_high, off_low = split(offset)
    half = jnp.concatenate([nrm_high, nrm_low, off_high, off_low], axis=0)
    return jnp.concatenate([half, half], axis=0).astype(BF16)

MESH = pl.DeviceIdType.MESH
NX, NY = 8, 16
DEVICES = NX * NY
PLACES = DEVICES * CAP
CHUNK = 8
EARLY = (64, 32)
PAIRS = 32
BODY = 8


def span(block):
    return pl.ds(pl.multiple_of(block * BLK, BLK), BLK)


def hops(offset):
    return sum((0, 1, 2, 1)[(offset >> bit) & 3] for bit in (1, 3, 5)) + 0.1 * (offset & 1)


ORDER = sorted(range(1, DEVICES), key=hops, reverse=True)


def partner(offset, mx, my):
    x = ((mx >> 1) + ((offset >> 5) & 3)) & 3
    y = ((my >> 2) + ((offset >> 3) & 3)) & 3
    z = ((my & 3) + ((offset >> 1) & 3)) & 3
    return 2 * x + ((mx & 1) ^ (offset & 1)), 4 * y + z


def bytes_wait(ref, sem):
    pltpu.make_async_copy(ref, ref, sem).wait()


def scatter_places(get, out, into, rows, sem_out, sem_in, mx, my):
    me = mx * NY + my

    for offset in ORDER:
        px, py = partner(offset, mx, my)
        to = px * NY + py
        for q in range(CAP):
            out[CAP * to + q] = get(CAP * to + q)
        pltpu.make_async_remote_copy(
            src_ref=out.at[pl.ds(CAP * to, CAP)],
            dst_ref=into.at[pl.ds(CAP * me, CAP)],
            send_sem=sem_out,
            recv_sem=sem_in,
            device_id=(px, py),
            device_id_type=MESH,
        ).start()
    for q in range(CAP):
        into[CAP * me + q] = get(CAP * me + q)


def neighbours(mx, my):
    devices = [
        ((mx + 1) & (NX - 1), my),
        ((mx - 1) & (NX - 1), my),
        (mx, (my + 1) & (NY - 1)),
        (mx, (my - 1) & (NY - 1)),
    ]
    return devices, [mx > 0, mx < NX - 1, my > 0, my < NY - 1]


def send_sides(source, target, sem_out, sem_in, devices):
    for side in range(4):
        pltpu.make_async_remote_copy(
            src_ref=source(side),
            dst_ref=target(side),
            send_sem=sem_out,
            recv_sem=sem_in,
            device_id=devices[side],
            device_id_type=MESH,
        ).start()


def contact_pairs(pairs_ref, start_ref, len_ref, node_tab, facet_tab, tile_out):
    facet = lax.broadcasted_iota(jnp.int32, (BLK, 2 * BLK), 0) << 25
    zero = jnp.zeros((16, BLK), BF16)
    top = jnp.int32(-(2**31))

    def pair(g, carry):
        t = 2 * g
        left = [facet_tab[pairs_ref[1, t + h]] for h in range(2)]
        right = [node_tab[pairs_ref[0, t + h]] for h in range(2)]
        depth = lax.dot_general(
            jnp.concatenate(left, axis=0),
            jnp.concatenate(
                [
                    jnp.concatenate([right[0], zero], axis=1),
                    jnp.concatenate([zero, right[1]], axis=1),
                ],
                axis=0,
            ),
            (((0,), (0,)), ((), ())),
            preferred_element_type=F32,
        )
        start = jnp.concatenate([start_ref[pl.ds(t + h, 1)] for h in range(2)], axis=1)
        length = jnp.concatenate([len_ref[pl.ds(t + h, 1)] for h in range(2)], axis=1)
        shifted = (start << 25) + top
        last = ((length - 1) << 25) + top
        inside = facet - shifted <= last
        pressure = jnp.where(inside, jnp.maximum(depth, 0.0), 0.0)
        high = pressure.astype(BF16)
        low = (pressure - high.astype(F32)).astype(BF16)
        force = lax.dot_general(
            jnp.concatenate(
                [jnp.concatenate([left[h], left[h]], axis=1) for h in range(2)], axis=0
            ),
            jnp.concatenate([high, low], axis=0),
            (((1,), (0,)), ((), ())),
            preferred_element_type=F32,
        )
        tile_out[pl.ds(pl.multiple_of(8 * t, 16), 8)] = force[0:8, 0:BLK]
        tile_out[pl.ds(pl.multiple_of(8 * t + 8, 8), 8)] = force[16:24, BLK : 2 * BLK]
        return carry

    lax.fori_loop(0, start_ref.shape[0] // 2, pair, 0, unroll=PAIRS)


def place_sums(count_ref, slave_ref, tile_out, box):
    tiles = slave_ref.shape[1]
    place = lax.broadcasted_iota(jnp.int32, (PLACES, tiles), 0)
    active = lax.broadcasted_iota(jnp.int32, (PLACES, tiles), 1) < count_ref[0]
    pick = jnp.where((place == slave_ref[0:1]) & active, -PENALTY / BLK, 0.0).astype(BF16)
    for c in range(3):
        total = tile_out[pl.ds(c, tiles, 8)] + tile_out[pl.ds(c + 3, tiles, 8)]
        high, low = split(total)
        both = jnp.dot(
            pick,
            jnp.concatenate([high.astype(BF16), low.astype(BF16)], axis=1),
            preferred_element_type=F32,
        )
        box[pl.ds(c, PLACES, 8)] = both[:, 0:BLK] + both[:, BLK : 2 * BLK]


def invert_lists(shared_ref, inverse):
    blocks = inverse.shape[1]
    block = lax.broadcasted_iota(jnp.int32, (blocks, BLK), 0)
    entry = (lax.broadcasted_iota(jnp.int32, (blocks, BLK), 1) + 1).astype(F32)
    lane = lax.broadcasted_iota(jnp.int32, (BLK, BLK), 0)
    for side in range(4):
        node = shared_ref[side : side + 1]
        found = lax.dot_general(
            jnp.where(block == (node >> 7), entry, 0.0).astype(BF16),
            jnp.where(lane == (node & (BLK - 1)), 1.0, 0.0).astype(BF16),
            (((1,), (1,)), ((), ())),
            preferred_element_type=F32,
        )
        inverse[side] = found.astype(jnp.int32) - 1


def crash_kernel(
    slot_ref,
    edge_ref,
    pairs_ref,
    count_ref,
    disp_hbm,
    vel_hbm,
    ref_hbm,
    nrm_hbm,
    mass_hbm,
    corner_hbm,
    stiff_hbm,
    limit_hbm,
    shared_hbm,
    slave_hbm,
    start_hbm,
    len_hbm,
    disp_ref,
    vel_ref,
    disp_in,
    vel_in,
    ref_ref,
    nrm_ref,
    mass_ref,
    corner_ref,
    limit_ref,
    shared_ref,
    slave_ref,
    start_ref,
    len_ref,
    stiff,
    surface,
    out6,
    got6,
    out3,
    got3,
    edge_out6,
    edge_in6,
    edge_out3,
    edge_in3,
    node_tab,
    facet_tab,
    tile_out,
    box,
    home_out,
    home,
    internal,
    force,
    side_out,
    near,
    inverse,
    back_vec,
    back_ref,
    load_sem,
    stiff_sem,
    sem_out,
    sem_in,
):
    mx, my = lax.axis_index("gx"), lax.axis_index("gy")
    blocks = internal.shape[0]
    edges = edge_out3.shape[0]
    devices, exists = neighbours(mx, my)

    def stiff_copy(chunk):
        where = pl.ds(pl.multiple_of(chunk * CHUNK * BLK, BLK), CHUNK * BLK)
        return pltpu.make_async_copy(
            stiff_hbm.at[:, :, where], stiff.at[:, :, where], stiff_sem.at[chunk]
        )

    loads = [
        pltpu.make_async_copy(source, target, load_sem.at[i])
        for i, (source, target) in enumerate(
            (
                (disp_hbm, disp_in),
                (ref_hbm, ref_ref),
                (nrm_hbm, nrm_ref),
                (shared_hbm, shared_ref),
                (corner_hbm, corner_ref),
                (limit_hbm, limit_ref),
                (vel_hbm, vel_in),
                (mass_hbm, mass_ref),
                (slave_hbm, slave_ref),
                (start_hbm, start_ref),
                (len_hbm, len_ref),
            )
        )
    ]
    for load in loads:
        load.start()
    barrier = pltpu.get_barrier_semaphore()

    for offset in ORDER:
        pl.semaphore_signal(
            barrier, inc=1, device_id=partner(offset, mx, my), device_id_type=MESH
        )
    for chunk in range(blocks // CHUNK):
        stiff_copy(chunk).start()
    place = lax.broadcasted_iota(jnp.int32, (1, PLACES), 1)
    back = jnp.full((1, PLACES), blocks, jnp.int32)
    for k in range(blocks):
        back = jnp.where(place == slot_ref[k], k, back)
    back_vec[...] = back
    back_copy = pltpu.make_async_copy(back_vec, back_ref, load_sem.at[11])
    back_copy.start()
    for load in loads[0:4]:
        load.wait()
    invert_lists(shared_ref, inverse)
    surface[blocks] = jnp.zeros((8, BLK), F32)

    def first_surface(k, carry):
        where = span(k)
        surface[k, 0:3] = ref_ref[:, where] + disp_in[0:3, where]
        surface[k, 3:6] = nrm_ref[:, where]
        return carry

    lax.fori_loop(0, blocks, first_surface, 0, unroll=8)
    back_copy.wait()
    pl.semaphore_wait(barrier, DEVICES - 1)

    for step in range(STEPS):
        disp, vel = (disp_in, vel_in) if step == 0 else (disp_ref, vel_ref)
        out, got = (out6, got6) if step == 0 else (out3, got3)
        edge_out, edge_in = (edge_out6, edge_in6) if step == 0 else (edge_out3, edge_in3)
        rows = 6 if step == 0 else 3
        phase = 4 * step
        scatter_places(
            lambda r: surface[back_ref[0, r]][0:rows],
            out,
            got,
            rows,
            sem_out.at[phase],
            sem_in.at[phase],
            mx,
            my,
        )

        def elements(k, carry):
            where = span(k)
            internal[k] = element_block(
                disp[:, where],
                corner_ref[:, where] & (BLK - 1),
                lambda i: stiff[i, :, where],
                limit_ref[pl.ds(k, 1)],
            )
            return carry

        if step == 0:
            for load in loads[4:]:
                load.wait()
            for chunk in range(blocks // CHUNK):
                stiff_copy(chunk).wait()
        lax.fori_loop(0, EARLY[step], elements, 0, unroll=BODY)

        bytes_wait(got.at[pl.ds(0, PLACES - CAP)], sem_in.at[phase])
        for e in range(edges):
            edge_out[e] = got[edge_ref[e]]
        send_sides(
            lambda side: edge_out,
            lambda side: edge_in.at[pl.ds(edges * side, edges)],
            sem_out.at[phase + 1],
            sem_in.at[phase + 1],
            devices,
        )

        def tables(r, carry):
            pos = got[r][0:3]
            node_tab[r] = node_table(pos)
            facet_tab[r] = facet_table(pos, got6[r][3:6])
            return carry

        lax.fori_loop(0, PLACES, tables, 0, unroll=4)
        bytes_wait(edge_in, sem_in.at[phase + 1])
        for side in range(4):
            for e in range(edges):
                at = edges * side + e
                pos = jnp.where(exists[side], edge_in[at][0:3], 0.0)
                nrm = jnp.where(exists[side], edge_in6[at][3:6], 0.0)
                facet_tab[PLACES + at] = facet_table(pos, nrm)
        contact_pairs(pairs_ref, start_ref, len_ref, node_tab, facet_tab, tile_out)
        place_sums(count_ref, slave_ref, tile_out, box)
        scatter_places(
            lambda r: box[pl.ds(pl.multiple_of(8 * r, 8), 8)][0:3],
            home_out.at[step],
            home.at[step],
            3,
            sem_out.at[phase + 2],
            sem_in.at[phase + 2],
            mx,
            my,
        )
        lax.fori_loop(EARLY[step], blocks, elements, 0, unroll=BODY)
        bytes_wait(home.at[step, pl.ds(0, PLACES - CAP)], sem_in.at[phase + 2])

        node = [jnp.broadcast_to(shared_ref[s : s + 1], (8, BLK)) for s in range(4)]
        none = jnp.zeros((5, BLK), F32)

        def nodal(k, found):
            contact = jnp.concatenate([home[step, slot_ref[k]], none], axis=0)
            total = contact - internal[k]
            force[k] = total
            return tuple(
                jnp.where((node[s] >> 7) == k, lanes(total, node[s] & (BLK - 1)), found[s])
                for s in range(4)
            )

        found = lax.fori_loop(
            0, blocks, nodal, tuple(jnp.zeros((8, BLK), F32) for s in range(4)), unroll=8
        )
        for s in range(4):
            side_out[step, s] = found[s][0:6]
        give = (1, 0, 3, 2)
        send_sides(
            lambda side: side_out.at[step, give[side]],
            lambda side: near.at[step, side],
            sem_out.at[phase + 3],
            sem_in.at[phase + 3],
            devices,
        )

        def advance(k, carry):
            where = span(k)
            vel_ref[:, where] = vel[:, where] + TIME_STEP * mass_ref[:, where] * force[k][0:6]
            return carry

        lax.fori_loop(0, blocks, advance, 0, unroll=8)
        bytes_wait(near.at[step], sem_in.at[phase + 3])
        given = [
            jnp.concatenate(
                [jnp.where(exists[s], near[step, s], 0.0), jnp.zeros((2, BLK), F32)], axis=0
            )
            for s in range(4)
        ]

        def assemble(k, carry):
            where = span(k)
            added = jnp.zeros((8, BLK), F32)
            for s in range(4):
                entry = jnp.broadcast_to(inverse[s, pl.ds(k, 1)], (8, BLK))
                added = added + jnp.where(entry >= 0, lanes(given[s], entry & (BLK - 1)), 0.0)
            speed = vel_ref[:, where] + TIME_STEP * mass_ref[:, where] * added[0:6]
            if step < STEPS - 1:
                moved = disp[:, where] + TIME_STEP * speed
                vel_ref[:, where] = speed
                disp_ref[:, where] = moved
                surface[k, 0:3] = ref_ref[:, where] + moved[0:3]
            else:
                vel_ref[:, where] = TIME_STEP * speed
            return carry

        lax.fori_loop(0, blocks, assemble, 0, unroll=8)

    for step in range(STEPS):
        phase = 4 * step
        out = out6 if step == 0 else out3
        edge_in = edge_in6 if step == 0 else edge_in3
        bytes_wait(out.at[pl.ds(0, PLACES - CAP)], sem_out.at[phase])
        bytes_wait(edge_in, sem_out.at[phase + 1])
        bytes_wait(home_out.at[step, pl.ds(0, PLACES - CAP)], sem_out.at[phase + 2])
        bytes_wait(near.at[step], sem_out.at[phase + 3])


def body(
    disp,
    vel,
    ref_pos,
    normals,
    mass,
    connectivity,
    stiffness,
    yield_force,
    shared,
    block_slot,
    edge_slots,
    tile_pairs,
    tile_count,
    win_start,
    win_len,
):
    blocks = disp.shape[1] // BLK
    tiles = win_start.shape[0]
    edges = edge_slots.shape[0]
    limit = yield_force.reshape(blocks, BLK)

    def vmem(*shape):
        return pltpu.VMEM(shape, F32)

    before, half = pl.pallas_call(
        crash_kernel,
        in_specs=[SMEM] * 4 + [pl.BlockSpec(memory_space=pl.ANY)] * 12,
        out_specs=[VMEM, VMEM],
        out_shape=[jax.ShapeDtypeStruct(disp.shape, F32)] * 2,
        scratch_shapes=[
            vmem(*disp.shape),
            vmem(*vel.shape),
            vmem(*ref_pos.shape),
            vmem(*normals.shape),
            vmem(*mass.shape),
            pltpu.VMEM(connectivity.shape, jnp.int32),
            vmem(*limit.shape),
            pltpu.VMEM(shared.shape, jnp.int32),
            pltpu.VMEM(tile_pairs.shape, jnp.int32),
            pltpu.VMEM(win_start.shape, jnp.int32),
            pltpu.VMEM(win_len.shape, jnp.int32),
            pltpu.VMEM(stiffness.shape, BF16),
            vmem(blocks + 1, 8, BLK),
            vmem(PLACES, 6, BLK),
            vmem(PLACES, 6, BLK),
            vmem(PLACES, 3, BLK),
            vmem(PLACES, 3, BLK),
            vmem(edges, 6, BLK),
            vmem(4 * edges, 6, BLK),
            vmem(edges, 3, BLK),
            vmem(4 * edges, 3, BLK),
            pltpu.VMEM((PLACES, 16, BLK), BF16),
            pltpu.VMEM((PLACES + 4 * edges, 16, BLK), BF16),
            vmem(8 * tiles, BLK),
            vmem(8 * PLACES, BLK),
            vmem(STEPS, PLACES, 3, BLK),
            vmem(STEPS, PLACES, 3, BLK),
            vmem(blocks, 8, BLK),
            vmem(blocks, 8, BLK),
            vmem(STEPS, 4, 6, BLK),
            vmem(STEPS, 4, 6, BLK),
            pltpu.VMEM((4, blocks, BLK), jnp.int32),
            pltpu.VMEM((1, PLACES), jnp.int32),
            pltpu.SMEM((1, PLACES), jnp.int32),
            pltpu.SemaphoreType.DMA((12,)),
            pltpu.SemaphoreType.DMA((blocks // CHUNK,)),
            pltpu.SemaphoreType.DMA((4 * STEPS,)),
            pltpu.SemaphoreType.DMA((4 * STEPS,)),
        ],
        compiler_params=pltpu.CompilerParams(
            vmem_limit_bytes=LIMIT, collective_id=0, has_side_effects=True
        ),
        name="crash_steps",
    )(
        block_slot,
        edge_slots,
        tile_pairs,
        tile_count,
        disp,
        vel,
        ref_pos,
        normals,
        mass,
        connectivity,
        stiffness,
        limit,
        shared,
        tile_pairs,
        win_start,
        win_len,
    )
    return before + half, half + half


def solution(mesh):
    row, flat, lead = P(None, ("gx", "gy")), P(("gx", "gy")), P(("gx", "gy"), None)
    placed = (row, row, row, row, row, row, P(None, None, ("gx", "gy")), flat)
    placed = placed + (row, flat, flat, row, flat, lead, lead)
    return jax.shard_map(
        body, mesh=mesh, in_specs=placed, out_specs=(row, row), check_vma=False
    )
```

```python
import jax
import jax.numpy as jnp
from jax import lax
from jax.experimental import pallas as pl
from jax.experimental.pallas import tpu as pltpu
from jax.sharding import PartitionSpec as P

BLK = 128
CAP = 2
STEPS = 2
TIME_STEP = 0.5
PENALTY = 32.0
THICKNESS = 0.2
F32 = jnp.float32
BF16 = jnp.bfloat16
VMEM = pl.BlockSpec(memory_space=pltpu.VMEM)
SMEM = pl.BlockSpec(memory_space=pltpu.SMEM)
LIMIT = 64 * 1024 * 1024 - 65536


def rows_iota():
    return lax.broadcasted_iota(jnp.int32, (8, BLK), 0)


def merge_rows(even, odd, bit):
    low = (rows_iota() & bit) == 0
    return jnp.where(low, even, odd) + pltpu.roll(jnp.where(low, odd, even), bit, 0)


def sum_six(parts):
    first = [merge_rows(parts[2 * m], parts[2 * m + 1], 1) for m in range(3)]
    upper = first[2] + pltpu.roll(first[2], 2, 0)
    return merge_rows(merge_rows(first[0], first[1], 2), upper, 4)


def split(value):
    high = value.astype(BF16).astype(F32)
    return high, value - high


def lanes(value, index):
    return jnp.take_along_axis(value, index, axis=1)


def element_block(disp, corner, load_stiff, limit):
    index = jnp.concatenate([corner, corner], axis=0)
    dofs = []
    for pair in range(3):
        source = jnp.concatenate(
            [
                jnp.broadcast_to(disp[2 * pair : 2 * pair + 1], (4, BLK)),
                jnp.broadcast_to(disp[2 * pair + 1 : 2 * pair + 2], (4, BLK)),
            ],
            axis=0,
        )
        dofs.append(lanes(source, index))
    trial = []
    for a in range(4):
        parts = []
        for c in range(6):
            row = load_stiff(4 * c + a).astype(F32)
            parts.append(row[0:8] * dofs[0] + row[8:16] * dofs[1] + row[16:24] * dofs[2])
        trial.append(sum_six(parts))
    squares = trial[0] * trial[0] + trial[1] * trial[1] + trial[2] * trial[2] + trial[3] * trial[3]
    squared = jnp.sum(jnp.where(rows_iota() < 6, squares, 0.0), axis=0, keepdims=True)
    factor = 1.0 / jnp.sqrt(1.0 + squared / (limit * limit))
    node = lax.broadcasted_iota(jnp.int32, (BLK, BLK), 0)
    left = []
    right = []
    for a in range(4):
        high, low = split(trial[a] * factor)
        left.append(jnp.concatenate([high, low], axis=0).astype(BF16))
        right.append(jnp.where(node == corner[a : a + 1], 1.0, 0.0).astype(BF16))
    both = lax.dot_general(
        jnp.concatenate(left, axis=1),
        jnp.concatenate(right, axis=1),
        (((1,), (1,)), ((), ())),
        preferred_element_type=F32,
    )
    return both[0:8] + both[8:16]


def node_table(pos):
    full = jnp.concatenate([pos, pos, jnp.ones((2, BLK), F32)], axis=0)
    high, low = split(full)
    return jnp.concatenate([high, low], axis=0).astype(BF16)


def facet_table(pos, nrm):
    offset = jnp.sum(pos * nrm, axis=0, keepdims=True) + THICKNESS
    nrm_high, nrm_low = split(-nrm)
    off_high, off_low = split(offset)
    half = jnp.concatenate([nrm_high, nrm_low, off_high, off_low], axis=0)
    return jnp.concatenate([half, half], axis=0).astype(BF16)

MESH = pl.DeviceIdType.MESH
NX, NY = 8, 16
DEVICES = NX * NY
PLACES = DEVICES * CAP
CHUNK = 8
EARLY = (48, 32)
PAIRS = 64
BODY = 8


def span(block):
    return pl.ds(pl.multiple_of(block * BLK, BLK), BLK)


def hops(offset):
    return sum((0, 1, 2, 1)[(offset >> bit) & 3] for bit in (1, 3, 5)) + 0.1 * (offset & 1)


ORDER = sorted(range(1, DEVICES), key=hops, reverse=True)


def partner(offset, mx, my):
    x = ((mx >> 1) + ((offset >> 5) & 3)) & 3
    y = ((my >> 2) + ((offset >> 3) & 3)) & 3
    z = ((my & 3) + ((offset >> 1) & 3)) & 3
    return 2 * x + ((mx & 1) ^ (offset & 1)), 4 * y + z


def bytes_wait(ref, sem):
    pltpu.make_async_copy(ref, ref, sem).wait()


def scatter_places(get, out, into, rows, sem_out, sem_in, mx, my):
    me = mx * NY + my

    for offset in ORDER:
        px, py = partner(offset, mx, my)
        to = px * NY + py
        for q in range(CAP):
            out[CAP * to + q] = get(CAP * to + q)
        pltpu.make_async_remote_copy(
            src_ref=out.at[pl.ds(CAP * to, CAP)],
            dst_ref=into.at[pl.ds(CAP * me, CAP)],
            send_sem=sem_out,
            recv_sem=sem_in,
            device_id=(px, py),
            device_id_type=MESH,
        ).start()
    for q in range(CAP):
        into[CAP * me + q] = get(CAP * me + q)


def neighbours(mx, my):
    devices = [
        ((mx + 1) & (NX - 1), my),
        ((mx - 1) & (NX - 1), my),
        (mx, (my + 1) & (NY - 1)),
        (mx, (my - 1) & (NY - 1)),
    ]
    return devices, [mx > 0, mx < NX - 1, my > 0, my < NY - 1]


def send_sides(source, target, sem_out, sem_in, devices):
    for side in range(4):
        pltpu.make_async_remote_copy(
            src_ref=source(side),
            dst_ref=target(side),
            send_sem=sem_out,
            recv_sem=sem_in,
            device_id=devices[side],
            device_id_type=MESH,
        ).start()


def window_masks(start_ref, len_ref, masks):
    facet = lax.broadcasted_iota(jnp.int32, (BLK, 2 * BLK), 0) << 25
    top = jnp.int32(-(2**31))

    def pair(g, carry):
        t = 2 * g
        start = jnp.concatenate([start_ref[pl.ds(t + h, 1)] for h in range(2)], axis=1)
        length = jnp.concatenate([len_ref[pl.ds(t + h, 1)] for h in range(2)], axis=1)
        inside = facet - ((start << 25) + top) <= ((length - 1) << 25) + top
        masks[g] = jnp.where(inside, 1.0, 0.0).astype(BF16)
        return carry

    lax.fori_loop(0, masks.shape[0], pair, 0, unroll=8)


def contact_pairs(pairs_ref, masks, node_tab, facet_tab, tile_out):
    zero = jnp.zeros((16, BLK), BF16)

    def pair(g, carry):
        t = 2 * g
        left = [facet_tab[pairs_ref[1, t + h]] for h in range(2)]
        right = [node_tab[pairs_ref[0, t + h]] for h in range(2)]
        depth = lax.dot_general(
            jnp.concatenate(left, axis=0),
            jnp.concatenate(
                [
                    jnp.concatenate([right[0], zero], axis=1),
                    jnp.concatenate([zero, right[1]], axis=1),
                ],
                axis=0,
            ),
            (((0,), (0,)), ((), ())),
            preferred_element_type=F32,
        )
        mask = masks[g]
        pressure = jnp.maximum(depth, 0.0)
        high = pressure.astype(BF16)
        low = (pressure - high.astype(F32)).astype(BF16) * mask
        high = high * mask
        force = lax.dot_general(
            jnp.concatenate(
                [jnp.concatenate([left[h], left[h]], axis=1) for h in range(2)], axis=0
            ),
            jnp.concatenate([high, low], axis=0),
            (((1,), (0,)), ((), ())),
            preferred_element_type=F32,
        )
        tile_out[pl.ds(pl.multiple_of(8 * t, 16), 8)] = force[0:8, 0:BLK]
        tile_out[pl.ds(pl.multiple_of(8 * t + 8, 8), 8)] = force[16:24, BLK : 2 * BLK]
        return carry

    lax.fori_loop(0, masks.shape[0], pair, 0, unroll=PAIRS)


def place_picks(count_ref, slave_ref, pick):
    place = lax.broadcasted_iota(jnp.int32, pick.shape, 0)
    active = lax.broadcasted_iota(jnp.int32, pick.shape, 1) < count_ref[0]
    chosen = (place == slave_ref[0:1]) & active
    pick[...] = jnp.where(chosen, -PENALTY / BLK, 0.0).astype(BF16)


def place_sums(pick, tile_out, box):
    tiles = pick.shape[1]
    for c in range(3):
        total = tile_out[pl.ds(c, tiles, 8)] + tile_out[pl.ds(c + 3, tiles, 8)]
        high, low = split(total)
        both = jnp.dot(
            pick[...],
            jnp.concatenate([high.astype(BF16), low.astype(BF16)], axis=1),
            preferred_element_type=F32,
        )
        box[pl.ds(c, PLACES, 8)] = both[:, 0:BLK] + both[:, BLK : 2 * BLK]


def invert_lists(shared_ref, inverse):
    blocks = inverse.shape[1]
    block = lax.broadcasted_iota(jnp.int32, (blocks, BLK), 0)
    entry = (lax.broadcasted_iota(jnp.int32, (blocks, BLK), 1) + 1).astype(F32)
    lane = lax.broadcasted_iota(jnp.int32, (BLK, BLK), 0)
    for side in range(4):
        node = shared_ref[side : side + 1]
        found = lax.dot_general(
            jnp.where(block == (node >> 7), entry, 0.0).astype(BF16),
            jnp.where(lane == (node & (BLK - 1)), 1.0, 0.0).astype(BF16),
            (((1,), (1,)), ((), ())),
            preferred_element_type=F32,
        )
        inverse[side] = found.astype(jnp.int32) - 1


def crash_kernel(
    slot_ref,
    edge_ref,
    pairs_ref,
    count_ref,
    disp_hbm,
    vel_hbm,
    ref_hbm,
    nrm_hbm,
    mass_hbm,
    corner_hbm,
    stiff_hbm,
    limit_hbm,
    shared_hbm,
    slave_hbm,
    start_hbm,
    len_hbm,
    disp_ref,
    vel_ref,
    disp_in,
    vel_in,
    ref_ref,
    nrm_ref,
    mass_ref,
    corner_ref,
    limit_ref,
    shared_ref,
    slave_ref,
    start_ref,
    len_ref,
    stiff,
    surface,
    out6,
    got6,
    out3,
    got3,
    edge_out6,
    edge_in6,
    edge_out3,
    edge_in3,
    node_tab,
    facet_tab,
    tile_out,
    box,
    home_out,
    home,
    internal,
    force,
    side_out,
    near,
    inverse,
    back_vec,
    back_ref,
    masks,
    pick,
    load_sem,
    stiff_sem,
    sem_out,
    sem_in,
):
    mx, my = lax.axis_index("gx"), lax.axis_index("gy")
    blocks = internal.shape[0]
    edges = edge_out3.shape[0]
    devices, exists = neighbours(mx, my)

    def stiff_copy(chunk):
        where = pl.ds(pl.multiple_of(chunk * CHUNK * BLK, BLK), CHUNK * BLK)
        return pltpu.make_async_copy(
            stiff_hbm.at[:, :, where], stiff.at[:, :, where], stiff_sem.at[chunk]
        )

    loads = [
        pltpu.make_async_copy(source, target, load_sem.at[i])
        for i, (source, target) in enumerate(
            (
                (disp_hbm, disp_in),
                (ref_hbm, ref_ref),
                (nrm_hbm, nrm_ref),
                (shared_hbm, shared_ref),
                (corner_hbm, corner_ref),
                (limit_hbm, limit_ref),
                (vel_hbm, vel_in),
                (mass_hbm, mass_ref),
                (slave_hbm, slave_ref),
                (start_hbm, start_ref),
                (len_hbm, len_ref),
            )
        )
    ]
    for load in loads:
        load.start()
    barrier = pltpu.get_barrier_semaphore()

    for offset in ORDER:
        pl.semaphore_signal(
            barrier, inc=1, device_id=partner(offset, mx, my), device_id_type=MESH
        )
    for chunk in range(blocks // CHUNK):
        stiff_copy(chunk).start()
    place = lax.broadcasted_iota(jnp.int32, (1, PLACES), 1)
    back = jnp.full((1, PLACES), blocks, jnp.int32)
    for k in range(blocks):
        back = jnp.where(place == slot_ref[k], k, back)
    back_vec[...] = back
    back_copy = pltpu.make_async_copy(back_vec, back_ref, load_sem.at[11])
    back_copy.start()
    for load in loads[0:4]:
        load.wait()
    invert_lists(shared_ref, inverse)
    surface[blocks] = jnp.zeros((8, BLK), F32)

    def first_surface(k, carry):
        where = span(k)
        surface[k, 0:3] = ref_ref[:, where] + disp_in[0:3, where]
        surface[k, 3:6] = nrm_ref[:, where]
        return carry

    lax.fori_loop(0, blocks, first_surface, 0, unroll=8)
    back_copy.wait()
    pl.semaphore_wait(barrier, DEVICES - 1)

    for step in range(STEPS):
        disp, vel = (disp_in, vel_in) if step == 0 else (disp_ref, vel_ref)
        out, got = (out6, got6) if step == 0 else (out3, got3)
        edge_out, edge_in = (edge_out6, edge_in6) if step == 0 else (edge_out3, edge_in3)
        rows = 6 if step == 0 else 3
        phase = 4 * step
        scatter_places(
            lambda r: surface[back_ref[0, r]][0:rows],
            out,
            got,
            rows,
            sem_out.at[phase],
            sem_in.at[phase],
            mx,
            my,
        )

        def elements(k, carry):
            where = span(k)
            internal[k] = element_block(
                disp[:, where],
                corner_ref[:, where] & (BLK - 1),
                lambda i: stiff[i, :, where],
                limit_ref[pl.ds(k, 1)],
            )
            return carry

        if step == 0:
            for load in loads[4:]:
                load.wait()
            for chunk in range(blocks // CHUNK):
                stiff_copy(chunk).wait()
            window_masks(start_ref, len_ref, masks)
            place_picks(count_ref, slave_ref, pick)
        lax.fori_loop(0, EARLY[step], elements, 0, unroll=BODY)

        bytes_wait(got.at[pl.ds(0, PLACES - CAP)], sem_in.at[phase])
        for e in range(edges):
            edge_out[e] = got[edge_ref[e]]
        send_sides(
            lambda side: edge_out,
            lambda side: edge_in.at[pl.ds(edges * side, edges)],
            sem_out.at[phase + 1],
            sem_in.at[phase + 1],
            devices,
        )

        def tables(r, carry):
            pos = got[r][0:3]
            node_tab[r] = node_table(pos)
            facet_tab[r] = facet_table(pos, got6[r][3:6])
            return carry

        lax.fori_loop(0, PLACES, tables, 0, unroll=4)
        bytes_wait(edge_in, sem_in.at[phase + 1])
        for side in range(4):
            for e in range(edges):
                at = edges * side + e
                pos = jnp.where(exists[side], edge_in[at][0:3], 0.0)
                nrm = jnp.where(exists[side], edge_in6[at][3:6], 0.0)
                facet_tab[PLACES + at] = facet_table(pos, nrm)
        contact_pairs(pairs_ref, masks, node_tab, facet_tab, tile_out)
        place_sums(pick, tile_out, box)
        scatter_places(
            lambda r: box[pl.ds(pl.multiple_of(8 * r, 8), 8)][0:3],
            home_out.at[step],
            home.at[step],
            3,
            sem_out.at[phase + 2],
            sem_in.at[phase + 2],
            mx,
            my,
        )
        lax.fori_loop(EARLY[step], blocks, elements, 0, unroll=BODY)
        bytes_wait(home.at[step, pl.ds(0, PLACES - CAP)], sem_in.at[phase + 2])

        node = [jnp.broadcast_to(shared_ref[s : s + 1], (8, BLK)) for s in range(4)]
        none = jnp.zeros((5, BLK), F32)

        def nodal(k, found):
            contact = jnp.concatenate([home[step, slot_ref[k]], none], axis=0)
            total = contact - internal[k]
            force[k] = total
            return tuple(
                jnp.where((node[s] >> 7) == k, lanes(total, node[s] & (BLK - 1)), found[s])
                for s in range(4)
            )

        found = lax.fori_loop(
            0, blocks, nodal, tuple(jnp.zeros((8, BLK), F32) for s in range(4)), unroll=8
        )
        for s in range(4):
            side_out[step, s] = found[s][0:6]
        give = (1, 0, 3, 2)
        send_sides(
            lambda side: side_out.at[step, give[side]],
            lambda side: near.at[step, side],
            sem_out.at[phase + 3],
            sem_in.at[phase + 3],
            devices,
        )

        def advance(k, carry):
            where = span(k)
            vel_ref[:, where] = vel[:, where] + TIME_STEP * mass_ref[:, where] * force[k][0:6]
            return carry

        lax.fori_loop(0, blocks, advance, 0, unroll=8)
        bytes_wait(near.at[step], sem_in.at[phase + 3])
        given = [
            jnp.concatenate(
                [jnp.where(exists[s], near[step, s], 0.0), jnp.zeros((2, BLK), F32)], axis=0
            )
            for s in range(4)
        ]

        def assemble(k, carry):
            where = span(k)
            added = jnp.zeros((8, BLK), F32)
            for s in range(4):
                entry = jnp.broadcast_to(inverse[s, pl.ds(k, 1)], (8, BLK))
                added = added + jnp.where(entry >= 0, lanes(given[s], entry & (BLK - 1)), 0.0)
            speed = vel_ref[:, where] + TIME_STEP * mass_ref[:, where] * added[0:6]
            if step < STEPS - 1:
                moved = disp[:, where] + TIME_STEP * speed
                vel_ref[:, where] = speed
                disp_ref[:, where] = moved
                surface[k, 0:3] = ref_ref[:, where] + moved[0:3]
            else:
                vel_ref[:, where] = TIME_STEP * speed
            return carry

        lax.fori_loop(0, blocks, assemble, 0, unroll=8)

    for step in range(STEPS):
        phase = 4 * step
        out = out6 if step == 0 else out3
        edge_in = edge_in6 if step == 0 else edge_in3
        bytes_wait(out.at[pl.ds(0, PLACES - CAP)], sem_out.at[phase])
        bytes_wait(edge_in, sem_out.at[phase + 1])
        bytes_wait(home_out.at[step, pl.ds(0, PLACES - CAP)], sem_out.at[phase + 2])
        bytes_wait(near.at[step], sem_out.at[phase + 3])


def body(
    disp,
    vel,
    ref_pos,
    normals,
    mass,
    connectivity,
    stiffness,
    yield_force,
    shared,
    block_slot,
    edge_slots,
    tile_pairs,
    tile_count,
    win_start,
    win_len,
):
    blocks = disp.shape[1] // BLK
    tiles = win_start.shape[0]
    edges = edge_slots.shape[0]
    limit = yield_force.reshape(blocks, BLK)

    def vmem(*shape):
        return pltpu.VMEM(shape, F32)

    before, half = pl.pallas_call(
        crash_kernel,
        in_specs=[SMEM] * 4 + [pl.BlockSpec(memory_space=pl.ANY)] * 12,
        out_specs=[VMEM, VMEM],
        out_shape=[jax.ShapeDtypeStruct(disp.shape, F32)] * 2,
        scratch_shapes=[
            vmem(*disp.shape),
            vmem(*vel.shape),
            vmem(*ref_pos.shape),
            vmem(*normals.shape),
            vmem(*mass.shape),
            pltpu.VMEM(connectivity.shape, jnp.int32),
            vmem(*limit.shape),
            pltpu.VMEM(shared.shape, jnp.int32),
            pltpu.VMEM(tile_pairs.shape, jnp.int32),
            pltpu.VMEM(win_start.shape, jnp.int32),
            pltpu.VMEM(win_len.shape, jnp.int32),
            pltpu.VMEM(stiffness.shape, BF16),
            vmem(blocks + 1, 8, BLK),
            vmem(PLACES, 6, BLK),
            vmem(PLACES, 6, BLK),
            vmem(PLACES, 3, BLK),
            vmem(PLACES, 3, BLK),
            vmem(edges, 6, BLK),
            vmem(4 * edges, 6, BLK),
            vmem(edges, 3, BLK),
            vmem(4 * edges, 3, BLK),
            pltpu.VMEM((PLACES, 16, BLK), BF16),
            pltpu.VMEM((PLACES + 4 * edges, 16, BLK), BF16),
            vmem(8 * tiles, BLK),
            vmem(8 * PLACES, BLK),
            vmem(STEPS, PLACES, 3, BLK),
            vmem(STEPS, PLACES, 3, BLK),
            vmem(blocks, 8, BLK),
            vmem(blocks, 8, BLK),
            vmem(STEPS, 4, 6, BLK),
            vmem(STEPS, 4, 6, BLK),
            pltpu.VMEM((4, blocks, BLK), jnp.int32),
            pltpu.VMEM((1, PLACES), jnp.int32),
            pltpu.SMEM((1, PLACES), jnp.int32),
            pltpu.VMEM((tiles // 2, BLK, 2 * BLK), BF16),
            pltpu.VMEM((PLACES, tiles), BF16),
            pltpu.SemaphoreType.DMA((12,)),
            pltpu.SemaphoreType.DMA((blocks // CHUNK,)),
            pltpu.SemaphoreType.DMA((4 * STEPS,)),
            pltpu.SemaphoreType.DMA((4 * STEPS,)),
        ],
        compiler_params=pltpu.CompilerParams(
            vmem_limit_bytes=LIMIT, collective_id=0, has_side_effects=True
        ),
        name="crash_steps",
    )(
        block_slot,
        edge_slots,
        tile_pairs,
        tile_count,
        disp,
        vel,
        ref_pos,
        normals,
        mass,
        connectivity,
        stiffness,
        limit,
        shared,
        tile_pairs,
        win_start,
        win_len,
    )
    return before + half, half + half


def solution(mesh):
    row, flat, lead = P(None, ("gx", "gy")), P(("gx", "gy")), P(("gx", "gy"), None)
    placed = (row, row, row, row, row, row, P(None, None, ("gx", "gy")), flat)
    placed = placed + (row, flat, flat, row, flat, lead, lead)
    return jax.shard_map(
        body, mesh=mesh, in_specs=placed, out_specs=(row, row), check_vma=False
    )
```

```python
import jax
import jax.numpy as jnp
from jax import lax
from jax.experimental import pallas as pl
from jax.experimental.pallas import tpu as pltpu
from jax.sharding import PartitionSpec as P

BLK = 128
CAP = 2
STEPS = 2
TIME_STEP = 0.5
PENALTY = 32.0
THICKNESS = 0.2
F32 = jnp.float32
BF16 = jnp.bfloat16
VMEM = pl.BlockSpec(memory_space=pltpu.VMEM)
SMEM = pl.BlockSpec(memory_space=pltpu.SMEM)
LIMIT = 64 * 1024 * 1024 - 65536


def rows_iota():
    return lax.broadcasted_iota(jnp.int32, (8, BLK), 0)


def merge_rows(even, odd, bit):
    low = (rows_iota() & bit) == 0
    return jnp.where(low, even, odd) + pltpu.roll(jnp.where(low, odd, even), bit, 0)


def sum_six(parts):
    first = [merge_rows(parts[2 * m], parts[2 * m + 1], 1) for m in range(3)]
    upper = first[2] + pltpu.roll(first[2], 2, 0)
    return merge_rows(merge_rows(first[0], first[1], 2), upper, 4)


def split(value):
    high = value.astype(BF16).astype(F32)
    return high, value - high


def lanes(value, index):
    return jnp.take_along_axis(value, index, axis=1)


def element_block(disp, corner, load_stiff, limit):
    index = jnp.concatenate([corner, corner], axis=0)
    dofs = []
    for pair in range(3):
        source = jnp.concatenate(
            [
                jnp.broadcast_to(disp[2 * pair : 2 * pair + 1], (4, BLK)),
                jnp.broadcast_to(disp[2 * pair + 1 : 2 * pair + 2], (4, BLK)),
            ],
            axis=0,
        )
        dofs.append(lanes(source, index))
    trial = []
    for a in range(4):
        parts = []
        for c in range(6):
            row = load_stiff(4 * c + a).astype(F32)
            parts.append(row[0:8] * dofs[0] + row[8:16] * dofs[1] + row[16:24] * dofs[2])
        trial.append(sum_six(parts))
    squares = trial[0] * trial[0] + trial[1] * trial[1] + trial[2] * trial[2] + trial[3] * trial[3]
    squared = jnp.sum(jnp.where(rows_iota() < 6, squares, 0.0), axis=0, keepdims=True)
    factor = 1.0 / jnp.sqrt(1.0 + squared / (limit * limit))
    node = lax.broadcasted_iota(jnp.int32, (BLK, BLK), 0)
    left = []
    right = []
    for a in range(4):
        high, low = split(trial[a] * factor)
        left.append(jnp.concatenate([high, low], axis=0).astype(BF16))
        right.append(jnp.where(node == corner[a : a + 1], 1.0, 0.0).astype(BF16))
    both = lax.dot_general(
        jnp.concatenate(left, axis=1),
        jnp.concatenate(right, axis=1),
        (((1,), (1,)), ((), ())),
        preferred_element_type=F32,
    )
    return both[0:8] + both[8:16]


def node_table(pos):
    full = jnp.concatenate([pos, pos, jnp.ones((2, BLK), F32)], axis=0)
    high, low = split(full)
    return jnp.concatenate([high, low], axis=0).astype(BF16)


def facet_table(pos, nrm):
    offset = jnp.sum(pos * nrm, axis=0, keepdims=True) + THICKNESS
    nrm_high, nrm_low = split(-nrm)
    off_high, off_low = split(offset)
    half = jnp.concatenate([nrm_high, nrm_low, off_high, off_low], axis=0)
    return jnp.concatenate([half, half], axis=0).astype(BF16)

MESH = pl.DeviceIdType.MESH
NX, NY = 8, 16
DEVICES = NX * NY
PLACES = DEVICES * CAP
CHUNK = 8
EARLY = (40, 24)
PAIRS = 64
BODY = 8


def span(block):
    return pl.ds(pl.multiple_of(block * BLK, BLK), BLK)


def hops(offset):
    return sum((0, 1, 2, 1)[(offset >> bit) & 3] for bit in (1, 3, 5)) + 0.1 * (offset & 1)


ORDER = sorted(range(1, DEVICES), key=hops, reverse=True)


def partner(offset, mx, my):
    x = ((mx >> 1) + ((offset >> 5) & 3)) & 3
    y = ((my >> 2) + ((offset >> 3) & 3)) & 3
    z = ((my & 3) + ((offset >> 1) & 3)) & 3
    return 2 * x + ((mx & 1) ^ (offset & 1)), 4 * y + z


def bytes_wait(ref, sem):
    pltpu.make_async_copy(ref, ref, sem).wait()


def scatter_places(get, out, into, rows, sem_out, sem_in, mx, my):
    me = mx * NY + my

    for offset in ORDER:
        px, py = partner(offset, mx, my)
        to = px * NY + py
        for q in range(CAP):
            out[CAP * to + q] = get(CAP * to + q)
        pltpu.make_async_remote_copy(
            src_ref=out.at[pl.ds(CAP * to, CAP)],
            dst_ref=into.at[pl.ds(CAP * me, CAP)],
            send_sem=sem_out,
            recv_sem=sem_in,
            device_id=(px, py),
            device_id_type=MESH,
        ).start()
    for q in range(CAP):
        into[CAP * me + q] = get(CAP * me + q)


def neighbours(mx, my):
    devices = [
        ((mx + 1) & (NX - 1), my),
        ((mx - 1) & (NX - 1), my),
        (mx, (my + 1) & (NY - 1)),
        (mx, (my - 1) & (NY - 1)),
    ]
    return devices, [mx > 0, mx < NX - 1, my > 0, my < NY - 1]


def send_sides(source, target, sem_out, sem_in, devices):
    for side in range(4):
        pltpu.make_async_remote_copy(
            src_ref=source(side),
            dst_ref=target(side),
            send_sem=sem_out,
            recv_sem=sem_in,
            device_id=devices[side],
            device_id_type=MESH,
        ).start()


def window_masks(start_ref, len_ref, masks):
    facet = lax.broadcasted_iota(jnp.int32, (BLK, 2 * BLK), 0) << 25
    top = jnp.int32(-(2**31))

    def pair(g, carry):
        t = 2 * g
        start = jnp.concatenate([start_ref[pl.ds(t + h, 1)] for h in range(2)], axis=1)
        length = jnp.concatenate([len_ref[pl.ds(t + h, 1)] for h in range(2)], axis=1)
        inside = facet - ((start << 25) + top) <= ((length - 1) << 25) + top
        masks[g] = jnp.where(inside, 1.0, 0.0).astype(BF16)
        return carry

    lax.fori_loop(0, masks.shape[0], pair, 0, unroll=8)


def contact_pairs(pairs_ref, masks, node_tab, facet_tab, tile_out):
    zero = jnp.zeros((16, BLK), BF16)
    first = lax.broadcasted_iota(jnp.int32, (16, BLK), 0) < 8

    def pair(g, carry):
        t = 2 * g
        left = [facet_tab[pairs_ref[1, t + h]] for h in range(2)]
        right = [node_tab[pairs_ref[0, t + h]] for h in range(2)]
        depth = lax.dot_general(
            jnp.concatenate(left, axis=0),
            jnp.concatenate(
                [
                    jnp.concatenate([right[0], zero], axis=1),
                    jnp.concatenate([zero, right[1]], axis=1),
                ],
                axis=0,
            ),
            (((0,), (0,)), ((), ())),
            preferred_element_type=F32,
        )
        mask = masks[g]
        pressure = jnp.maximum(depth, 0.0)
        high = pressure.astype(BF16)
        low = (pressure - high.astype(F32)).astype(BF16) * mask
        high = high * mask
        normal = jnp.where(first, left[0], left[1])
        force = lax.dot_general(
            jnp.concatenate([normal, normal], axis=1),
            jnp.concatenate([high, low], axis=0),
            (((1,), (0,)), ((), ())),
            preferred_element_type=F32,
        )
        tile_out[pl.ds(pl.multiple_of(8 * t, 16), 8)] = force[0:8, 0:BLK]
        tile_out[pl.ds(pl.multiple_of(8 * t + 8, 8), 8)] = force[8:16, BLK : 2 * BLK]
        return carry

    lax.fori_loop(0, masks.shape[0], pair, 0, unroll=PAIRS)


def place_picks(count_ref, slave_ref, pick):
    place = lax.broadcasted_iota(jnp.int32, pick.shape, 0)
    active = lax.broadcasted_iota(jnp.int32, pick.shape, 1) < count_ref[0]
    chosen = (place == slave_ref[0:1]) & active
    pick[...] = jnp.where(chosen, -PENALTY / BLK, 0.0).astype(BF16)


def place_sums(pick, tile_out, box):
    tiles = pick.shape[1]
    for c in range(3):
        total = tile_out[pl.ds(c, tiles, 8)] + tile_out[pl.ds(c + 3, tiles, 8)]
        high, low = split(total)
        both = jnp.dot(
            pick[...],
            jnp.concatenate([high.astype(BF16), low.astype(BF16)], axis=1),
            preferred_element_type=F32,
        )
        box[pl.ds(c, PLACES, 8)] = both[:, 0:BLK] + both[:, BLK : 2 * BLK]


def invert_lists(shared_ref, inverse):
    blocks = inverse.shape[1]
    block = lax.broadcasted_iota(jnp.int32, (blocks, BLK), 0)
    entry = (lax.broadcasted_iota(jnp.int32, (blocks, BLK), 1) + 1).astype(F32)
    lane = lax.broadcasted_iota(jnp.int32, (BLK, BLK), 0)
    for side in range(4):
        node = shared_ref[side : side + 1]
        found = lax.dot_general(
            jnp.where(block == (node >> 7), entry, 0.0).astype(BF16),
            jnp.where(lane == (node & (BLK - 1)), 1.0, 0.0).astype(BF16),
            (((1,), (1,)), ((), ())),
            preferred_element_type=F32,
        )
        inverse[side] = found.astype(jnp.int32) - 1


def crash_kernel(
    slot_ref,
    edge_ref,
    pairs_ref,
    count_ref,
    disp_hbm,
    vel_hbm,
    ref_hbm,
    nrm_hbm,
    mass_hbm,
    corner_hbm,
    stiff_hbm,
    limit_hbm,
    shared_hbm,
    slave_hbm,
    start_hbm,
    len_hbm,
    disp_ref,
    vel_ref,
    disp_in,
    vel_in,
    ref_ref,
    nrm_ref,
    mass_ref,
    corner_ref,
    limit_ref,
    shared_ref,
    slave_ref,
    start_ref,
    len_ref,
    stiff,
    surface,
    out6,
    got6,
    out3,
    got3,
    edge_out6,
    edge_in6,
    edge_out3,
    edge_in3,
    node_tab,
    facet_tab,
    tile_out,
    box,
    home_out,
    home,
    internal,
    force,
    side_out,
    near,
    inverse,
    back_vec,
    back_ref,
    masks,
    pick,
    load_sem,
    stiff_sem,
    sem_out,
    sem_in,
):
    mx, my = lax.axis_index("gx"), lax.axis_index("gy")
    blocks = internal.shape[0]
    edges = edge_out3.shape[0]
    devices, exists = neighbours(mx, my)

    def stiff_copy(chunk):
        where = pl.ds(pl.multiple_of(chunk * CHUNK * BLK, BLK), CHUNK * BLK)
        return pltpu.make_async_copy(
            stiff_hbm.at[:, :, where], stiff.at[:, :, where], stiff_sem.at[chunk]
        )

    barrier = pltpu.get_barrier_semaphore()

    for offset in ORDER:
        pl.semaphore_signal(
            barrier, inc=1, device_id=partner(offset, mx, my), device_id_type=MESH
        )
    loads = [
        pltpu.make_async_copy(source, target, load_sem.at[i])
        for i, (source, target) in enumerate(
            (
                (disp_hbm, disp_in),
                (ref_hbm, ref_ref),
                (nrm_hbm, nrm_ref),
                (shared_hbm, shared_ref),
                (corner_hbm, corner_ref),
                (limit_hbm, limit_ref),
                (vel_hbm, vel_in),
                (mass_hbm, mass_ref),
                (slave_hbm, slave_ref),
                (start_hbm, start_ref),
                (len_hbm, len_ref),
            )
        )
    ]
    for load in loads:
        load.start()
    for chunk in range(blocks // CHUNK):
        stiff_copy(chunk).start()
    place = lax.broadcasted_iota(jnp.int32, (1, PLACES), 1)
    back = jnp.full((1, PLACES), blocks, jnp.int32)
    for k in range(blocks):
        back = jnp.where(place == slot_ref[k], k, back)
    back_vec[...] = back
    back_copy = pltpu.make_async_copy(back_vec, back_ref, load_sem.at[11])
    back_copy.start()
    for load in loads[0:4]:
        load.wait()
    invert_lists(shared_ref, inverse)
    surface[blocks] = jnp.zeros((8, BLK), F32)

    def first_surface(k, carry):
        where = span(k)
        surface[k, 0:3] = ref_ref[:, where] + disp_in[0:3, where]
        surface[k, 3:6] = nrm_ref[:, where]
        return carry

    lax.fori_loop(0, blocks, first_surface, 0, unroll=8)
    back_copy.wait()
    pl.semaphore_wait(barrier, DEVICES - 1)

    for step in range(STEPS):
        disp, vel = (disp_in, vel_in) if step == 0 else (disp_ref, vel_ref)
        out, got = (out6, got6) if step == 0 else (out3, got3)
        edge_out, edge_in = (edge_out6, edge_in6) if step == 0 else (edge_out3, edge_in3)
        rows = 6 if step == 0 else 3
        phase = 4 * step
        scatter_places(
            lambda r: surface[back_ref[0, r]][0:rows],
            out,
            got,
            rows,
            sem_out.at[phase],
            sem_in.at[phase],
            mx,
            my,
        )

        def elements(k, carry):
            where = span(k)
            internal[k] = element_block(
                disp[:, where],
                corner_ref[:, where] & (BLK - 1),
                lambda i: stiff[i, :, where],
                limit_ref[pl.ds(k, 1)],
            )
            return carry

        if step == 0:
            for load in loads[4:]:
                load.wait()
            for chunk in range(blocks // CHUNK):
                stiff_copy(chunk).wait()
            window_masks(start_ref, len_ref, masks)
            place_picks(count_ref, slave_ref, pick)
        lax.fori_loop(0, EARLY[step], elements, 0, unroll=BODY)

        bytes_wait(got.at[pl.ds(0, PLACES - CAP)], sem_in.at[phase])
        for e in range(edges):
            edge_out[e] = got[edge_ref[e]]
        send_sides(
            lambda side: edge_out,
            lambda side: edge_in.at[pl.ds(edges * side, edges)],
            sem_out.at[phase + 1],
            sem_in.at[phase + 1],
            devices,
        )

        def tables(r, carry):
            pos = got[r][0:3]
            node_tab[r] = node_table(pos)
            facet_tab[r] = facet_table(pos, got6[r][3:6])
            return carry

        lax.fori_loop(0, PLACES, tables, 0, unroll=16)
        bytes_wait(edge_in, sem_in.at[phase + 1])
        for side in range(4):
            for e in range(edges):
                at = edges * side + e
                pos = jnp.where(exists[side], edge_in[at][0:3], 0.0)
                nrm = jnp.where(exists[side], edge_in6[at][3:6], 0.0)
                facet_tab[PLACES + at] = facet_table(pos, nrm)
        contact_pairs(pairs_ref, masks, node_tab, facet_tab, tile_out)
        place_sums(pick, tile_out, box)
        scatter_places(
            lambda r: box[pl.ds(pl.multiple_of(8 * r, 8), 8)][0:3],
            home_out.at[step],
            home.at[step],
            3,
            sem_out.at[phase + 2],
            sem_in.at[phase + 2],
            mx,
            my,
        )
        lax.fori_loop(EARLY[step], blocks, elements, 0, unroll=BODY)
        bytes_wait(home.at[step, pl.ds(0, PLACES - CAP)], sem_in.at[phase + 2])

        node = [jnp.broadcast_to(shared_ref[s : s + 1], (8, BLK)) for s in range(4)]
        none = jnp.zeros((5, BLK), F32)

        def nodal(k, found):
            contact = jnp.concatenate([home[step, slot_ref[k]], none], axis=0)
            total = contact - internal[k]
            force[k] = total
            return tuple(
                jnp.where((node[s] >> 7) == k, lanes(total, node[s] & (BLK - 1)), found[s])
                for s in range(4)
            )

        found = lax.fori_loop(
            0, blocks, nodal, tuple(jnp.zeros((8, BLK), F32) for s in range(4)), unroll=16
        )
        for s in range(4):
            side_out[step, s] = found[s][0:6]
        give = (1, 0, 3, 2)
        send_sides(
            lambda side: side_out.at[step, give[side]],
            lambda side: near.at[step, side],
            sem_out.at[phase + 3],
            sem_in.at[phase + 3],
            devices,
        )

        def advance(k, carry):
            where = span(k)
            vel_ref[:, where] = vel[:, where] + TIME_STEP * mass_ref[:, where] * force[k][0:6]
            return carry

        lax.fori_loop(0, blocks, advance, 0, unroll=8)
        bytes_wait(near.at[step], sem_in.at[phase + 3])
        given = [
            jnp.concatenate(
                [jnp.where(exists[s], near[step, s], 0.0), jnp.zeros((2, BLK), F32)], axis=0
            )
            for s in range(4)
        ]

        def assemble(k, carry):
            where = span(k)
            added = jnp.zeros((8, BLK), F32)
            for s in range(4):
                entry = jnp.broadcast_to(inverse[s, pl.ds(k, 1)], (8, BLK))
                added = added + jnp.where(entry >= 0, lanes(given[s], entry & (BLK - 1)), 0.0)
            speed = vel_ref[:, where] + TIME_STEP * mass_ref[:, where] * added[0:6]
            if step < STEPS - 1:
                moved = disp[:, where] + TIME_STEP * speed
                vel_ref[:, where] = speed
                disp_ref[:, where] = moved
                surface[k, 0:3] = ref_ref[:, where] + moved[0:3]
            else:
                vel_ref[:, where] = TIME_STEP * speed
            return carry

        lax.fori_loop(0, blocks, assemble, 0, unroll=16)

    for step in range(STEPS):
        phase = 4 * step
        out = out6 if step == 0 else out3
        edge_in = edge_in6 if step == 0 else edge_in3
        bytes_wait(out.at[pl.ds(0, PLACES - CAP)], sem_out.at[phase])
        bytes_wait(edge_in, sem_out.at[phase + 1])
        bytes_wait(home_out.at[step, pl.ds(0, PLACES - CAP)], sem_out.at[phase + 2])
        bytes_wait(near.at[step], sem_out.at[phase + 3])


def body(
    disp,
    vel,
    ref_pos,
    normals,
    mass,
    connectivity,
    stiffness,
    yield_force,
    shared,
    block_slot,
    edge_slots,
    tile_pairs,
    tile_count,
    win_start,
    win_len,
):
    blocks = disp.shape[1] // BLK
    tiles = win_start.shape[0]
    edges = edge_slots.shape[0]
    limit = yield_force.reshape(blocks, BLK)

    def vmem(*shape):
        return pltpu.VMEM(shape, F32)

    before, half = pl.pallas_call(
        crash_kernel,
        in_specs=[SMEM] * 4 + [pl.BlockSpec(memory_space=pl.ANY)] * 12,
        out_specs=[VMEM, VMEM],
        out_shape=[jax.ShapeDtypeStruct(disp.shape, F32)] * 2,
        scratch_shapes=[
            vmem(*disp.shape),
            vmem(*vel.shape),
            vmem(*ref_pos.shape),
            vmem(*normals.shape),
            vmem(*mass.shape),
            pltpu.VMEM(connectivity.shape, jnp.int32),
            vmem(*limit.shape),
            pltpu.VMEM(shared.shape, jnp.int32),
            pltpu.VMEM(tile_pairs.shape, jnp.int32),
            pltpu.VMEM(win_start.shape, jnp.int32),
            pltpu.VMEM(win_len.shape, jnp.int32),
            pltpu.VMEM(stiffness.shape, BF16),
            vmem(blocks + 1, 8, BLK),
            vmem(PLACES, 6, BLK),
            vmem(PLACES, 6, BLK),
            vmem(PLACES, 3, BLK),
            vmem(PLACES, 3, BLK),
            vmem(edges, 6, BLK),
            vmem(4 * edges, 6, BLK),
            vmem(edges, 3, BLK),
            vmem(4 * edges, 3, BLK),
            pltpu.VMEM((PLACES, 16, BLK), BF16),
            pltpu.VMEM((PLACES + 4 * edges, 16, BLK), BF16),
            vmem(8 * tiles, BLK),
            vmem(8 * PLACES, BLK),
            vmem(STEPS, PLACES, 3, BLK),
            vmem(STEPS, PLACES, 3, BLK),
            vmem(blocks, 8, BLK),
            vmem(blocks, 8, BLK),
            vmem(STEPS, 4, 6, BLK),
            vmem(STEPS, 4, 6, BLK),
            pltpu.VMEM((4, blocks, BLK), jnp.int32),
            pltpu.VMEM((1, PLACES), jnp.int32),
            pltpu.SMEM((1, PLACES), jnp.int32),
            pltpu.VMEM((tiles // 2, BLK, 2 * BLK), BF16),
            pltpu.VMEM((PLACES, tiles), BF16),
            pltpu.SemaphoreType.DMA((12,)),
            pltpu.SemaphoreType.DMA((blocks // CHUNK,)),
            pltpu.SemaphoreType.DMA((4 * STEPS,)),
            pltpu.SemaphoreType.DMA((4 * STEPS,)),
        ],
        compiler_params=pltpu.CompilerParams(
            vmem_limit_bytes=LIMIT, collective_id=0, has_side_effects=True
        ),
        name="crash_steps",
    )(
        block_slot,
        edge_slots,
        tile_pairs,
        tile_count,
        disp,
        vel,
        ref_pos,
        normals,
        mass,
        connectivity,
        stiffness,
        limit,
        shared,
        tile_pairs,
        win_start,
        win_len,
    )
    return before + half, half + half


def solution(mesh):
    row, flat, lead = P(None, ("gx", "gy")), P(("gx", "gy")), P(("gx", "gy"), None)
    placed = (row, row, row, row, row, row, P(None, None, ("gx", "gy")), flat)
    placed = placed + (row, flat, flat, row, flat, lead, lead)
    return jax.shard_map(
        body, mesh=mesh, in_specs=placed, out_specs=(row, row), check_vma=False
    )
```
